128 devices in a mesh: sub: 16 (over y, x), blk: 8 (over z, core).
Axes of the slice: x: 4, y: 4, z: 4, core: 2. Of those that a mesh axis runs over, the one named last changes fastest.
Arguments:
- f_local: float32 [256, 16, 1024], P(('sub', 'blk')), may hold values from -6 to 6
- schur: float32 [256, 1024, 1024], P(('sub', 'blk')), as said below
- precond: float32 [256, 1024, 1024], P(('sub', 'blk')), as said below
- modes: float32 [256, 6, 1024], P(('sub', 'blk')), may hold values from -0.1875 to 0.1875
- coarse_inv: float32 [1536, 1536], P(('sub', 'blk')), as said below
- nbr_sub: int32 [256, 8], P(('sub', 'blk')), may hold values from -1 to 255, as said below
- nbr_blk: int32 [256, 8], P(('sub', 'blk')), may hold values from -1 to 7, as said below
Outputs:
- lambda_sol: float32 [256, 16, 1024], P(('sub', 'blk'))
- proj_residual: float32 [256, 16, 1024], P(('sub', 'blk'))
The draws below stay inside these ranges and needn't reach their ends.
Inputs may be any that keep to these rules, and one draw needn't show every extreme that they name: `nbr_sub`: sharing is mutual: if block j of subdomain s names block j2 of subdomain s2, that block names block j of s. The partner lies on the device next along sub or next along blk (either way, cyclic), with subdomains numbered in device order; each such pair of devices shares 1 to 4 blocks, and some pair shares exactly 4. `nbr_blk`: -1 exactly where nbr_sub is -1. `schur`: each subdomain's matrix is symmetric positive definite. `precond`: each subdomain's matrix is symmetric positive definite. `coarse_inv`: symmetric positive definite.
All inputs are finite; a program needn't handle non-finite values.
Results may differ from the reference program's by a relative error of at most 0.00017.
Values sent between devices are 32-bit elements; how exact they have to be, the bound alone decides.
A program may use at most 64 MiB of HBM per device.

```python
import math
import jax
import jax.numpy as jnp
from jax import lax

NB = 1024
MODES = 6
CASES = 16
ITERS = 2
CAP = 4
S_DEV = 2
NBLK = 8
NSUB = 256
NC = 1536
N_SUB = 16
N_BLK = 8


def pairing(key):
    slots_dev = S_DEV * NBLK
    key_sub, key_blk, key_order = jax.random.split(key, 3)
    count_sub = jax.random.randint(key_sub, (N_SUB, N_BLK), 1, CAP + 1).at[0, 0].set(CAP)
    count_blk = jax.random.randint(key_blk, (N_SUB, N_BLK), 1, CAP + 1).at[0, 0].set(CAP)
    scores = jax.random.randint(key_order, (N_SUB, N_BLK, slots_dev), 0, 1 << 20) * slots_dev + jnp.arange(slots_dev, dtype=jnp.int32)
    order = jnp.argsort(scores, axis=2).astype(jnp.int32)
    position = jnp.argsort(order, axis=2).astype(jnp.int32)
    first_end = count_sub
    second_end = first_end + jnp.roll(count_sub, 1, axis=0)
    third_end = second_end + count_blk
    fourth_end = third_end + jnp.roll(count_blk, 1, axis=1)
    grid_sub = jnp.arange(N_SUB, dtype=jnp.int32)[:, None, None] + jnp.zeros((1, N_BLK, slots_dev), jnp.int32)
    grid_blk = jnp.arange(N_BLK, dtype=jnp.int32)[None, :, None] + jnp.zeros((N_SUB, 1, slots_dev), jnp.int32)
    first_here = first_end[:, :, None]
    second_here = second_end[:, :, None]
    third_here = third_end[:, :, None]
    fourth_here = fourth_end[:, :, None]
    first_next = jnp.roll(first_end, -1, axis=0)[:, :, None]
    third_next = jnp.roll(third_end, -1, axis=1)[:, :, None]
    second_prev = jnp.roll(second_end, 1, axis=1)[:, :, None]
    group_zero = position < first_here
    group_one = (position >= first_here) & (position < second_here)
    group_two = (position >= second_here) & (position < third_here)
    group_three = (position >= third_here) & (position < fourth_here)
    paired = group_zero | group_one | group_two | group_three
    partner_sub = jnp.where(group_zero, (grid_sub + 1) % N_SUB, jnp.where(group_one, (grid_sub + N_SUB - 1) % N_SUB, grid_sub))
    partner_blk = jnp.where(group_two, (grid_blk + 1) % N_BLK, jnp.where(group_three, (grid_blk + N_BLK - 1) % N_BLK, grid_blk))
    partner_pos = jnp.where(group_zero, first_next + position, jnp.where(group_one, position - first_here, jnp.where(group_two, third_next + position - second_here, jnp.where(group_three, second_prev + position - third_here, 0))))
    partner_pos = jnp.clip(partner_pos, 0, slots_dev - 1)
    partner_slot = order[partner_sub, partner_blk, partner_pos]
    partner_dev = partner_sub * N_BLK + partner_blk
    global_sub = partner_dev * S_DEV + partner_slot // NBLK
    global_blk = partner_slot % NBLK
    global_sub = jnp.where(paired, global_sub, -1).astype(jnp.int32)
    global_blk = jnp.where(paired, global_blk, -1).astype(jnp.int32)
    return (global_sub.reshape(NSUB, NBLK), global_blk.reshape(NSUB, NBLK))


def symmetric(key, count, order_size, low, high):
    key_diag, key_off = jax.random.split(key)
    diagonal = jnp.exp(jax.random.uniform(key_diag, (count, order_size), jnp.float32, math.log(low), math.log(high)))
    noise = jax.random.uniform(key_off, (count, order_size, order_size), jnp.float32, -1.0, 1.0)
    mixed = (noise + jnp.swapaxes(noise, 1, 2)) * (0.3 * order_size ** (-0.5)) + jnp.eye(order_size, dtype=jnp.float32)[None]
    root = jnp.sqrt(diagonal)
    scaling = root[:, :, None] * root[:, None, :]
    return mixed * scaling


def draw_nbr_sub(key, part):
    return pairing(key)[0]


def draw_nbr_blk(key, part):
    return pairing(key)[1]


def draw_schur(key, part):
    key = jax.random.fold_in(key, 11)
    return symmetric(key, NSUB, NB, 0.5, 4.0)


def draw_precond(key, part):
    key = jax.random.fold_in(key, 12)
    return symmetric(key, NSUB, NB, 0.25, 2.0)


def draw_coarse_inv(key, part):
    key = jax.random.fold_in(key, 13)
    return symmetric(key, 1, NC, 0.3, 0.6)[0]


def levels(rng, shape, pieces, least, top_value):
    def one(dim, shards_of):
        heights = jax.random.uniform(jax.random.fold_in(jax.random.fold_in(rng, 6), dim), (shards_of,), jnp.float32, least / len(pieces), top_value / len(pieces))
        return jnp.repeat(jnp.exp(heights), shape[dim] // shards_of).reshape((-1,) + (1,) * (len(shape) - dim - 1))

    level = one(*pieces[0])
    for cut in pieces[1:]:
        level = level * one(*cut)
    return level


def bell_draw(own_key, shape, width, most, shards=(), kind=jnp.bfloat16):
    gain = levels(own_key, shape, shards, -0.22, 0.18) if shards else 1.0
    drawn = jax.random.normal(own_key, shape, jnp.float32) * width * gain
    return jnp.minimum(jnp.maximum(drawn, -most), most).astype(kind)


def setup_inputs(seed: int = 0) -> dict:
    arg_keys = jax.random.split(jax.random.key(seed), 8)
    return {
        "f_local": bell_draw(arg_keys[0], (NSUB, CASES, NB), 1.0, 6.0, ((0, 128),), jnp.float32),
        "schur": draw_schur(jax.random.fold_in(arg_keys[7], 71), 0),
        "precond": draw_precond(jax.random.fold_in(arg_keys[7], 71), 0),
        "modes": bell_draw(arg_keys[3], (NSUB, MODES, NB), NB ** -0.5, 0.1875, ((0, 128),), jnp.float32),
        "coarse_inv": draw_coarse_inv(jax.random.fold_in(arg_keys[7], 71), 0),
        "nbr_sub": draw_nbr_sub(jax.random.fold_in(arg_keys[7], 71), 0),
        "nbr_blk": draw_nbr_blk(jax.random.fold_in(arg_keys[7], 71), 0),
    }


def assemble(values, nbr_sub, nbr_blk):
    num_sub, num_cases, num_width = values.shape
    num_blocks = nbr_sub.shape[1]
    blocks = values.reshape(num_sub, num_cases, num_blocks, num_width // num_blocks)
    paired = nbr_sub >= 0
    partner_rows = jnp.where(paired, nbr_sub, 0).astype(jnp.int32)
    partner_cols = jnp.where(paired, nbr_blk, 0).astype(jnp.int32)
    partner = blocks[partner_rows, :, partner_cols, :]
    partner = jnp.transpose(partner, (0, 2, 1, 3)) * paired.astype(jnp.float32)[:, None, :, None]
    return (blocks - partner).reshape(values.shape)


def weighted_dot(left, right, nbr_sub):
    num_sub, num_cases, num_width = left.shape
    num_blocks = nbr_sub.shape[1]
    per_block = jnp.sum((left * right).reshape(num_sub, num_cases, num_blocks, num_width // num_blocks), axis=3)
    weights = jnp.where(nbr_sub >= 0, 0.5, 1.0).astype(jnp.float32)
    return jnp.sum(per_block * weights[:, None, :], axis=(0, 2))


def project(values, modes, coarse_inv, nbr_sub, nbr_blk):
    num_sub, num_cases, num_width = values.shape
    moments = jnp.einsum("smn,scn->csm", modes, values, precision=lax.Precision.HIGHEST).reshape(num_cases, -1)
    factors = jnp.einsum("kn,cn->ck", coarse_inv, moments, precision=lax.Precision.HIGHEST)
    spread = jnp.einsum("smn,csm->scn", modes, factors.reshape(num_cases, num_sub, modes.shape[1]), precision=lax.Precision.HIGHEST)
    return values - assemble(spread, nbr_sub, nbr_blk)


def apply_local(matrices, values):
    return jnp.einsum("sij,scj->sci", matrices, values, precision=lax.Precision.HIGHEST)


def reference(f_local, schur, precond, modes, coarse_inv, nbr_sub, nbr_blk):
    residual = assemble(f_local, nbr_sub, nbr_blk)
    proj_residual = project(residual, modes, coarse_inv, nbr_sub, nbr_blk)
    lambda_sol = jnp.zeros_like(f_local)
    direction = jnp.zeros_like(f_local)
    rho_before = jnp.ones((f_local.shape[1],), jnp.float32)
    for iteration in range(ITERS):
        precond_out = assemble(apply_local(precond, proj_residual), nbr_sub, nbr_blk)
        search = project(precond_out, modes, coarse_inv, nbr_sub, nbr_blk)
        rho_now = weighted_dot(search, residual, nbr_sub)
        if iteration == 0:
            direction = search
        else:
            direction = search + (rho_now / rho_before)[None, :, None] * direction
        image = assemble(apply_local(schur, direction), nbr_sub, nbr_blk)
        sigma_now = weighted_dot(direction, image, nbr_sub)
        step_size = (rho_now / sigma_now)[None, :, None]
        lambda_sol = lambda_sol + step_size * direction
        residual = residual - step_size * image
        proj_residual = project(residual, modes, coarse_inv, nbr_sub, nbr_blk)
        rho_before = rho_now
    return lambda_sol, proj_residual
```

```python
import jax
import jax.numpy as jnp
from jax import lax
from jax.experimental import pallas as pl
from jax.experimental.pallas import tpu as pltpu
from jax.sharding import PartitionSpec as P

ITERS = 2
GATHERS = 1 + 2 * ITERS
SWAPS = 2 * ITERS
NSUB_AX, NBLK_AX = 16, 8
ROWS = 80
MESH = pl.DeviceIdType.MESH
F32, BF16 = jnp.float32, jnp.bfloat16


def split(x):
    hi = x.astype(BF16)
    return hi, (x - hi.astype(F32)).astype(BF16)


def dot(a, b):
    return jnp.dot(a, b, preferred_element_type=F32)


def dot_t(a, b):
    return lax.dot_general(a, b, (((1,), (1,)), ((), ())), preferred_element_type=F32)


def product3(x, hi, lo, mul=dot):
    rows = x.shape[0]
    xh, xl = split(x)
    both = mul(jnp.concatenate([xh, xl], axis=0), hi)
    return both[:rows] + both[rows:] + mul(xh, lo)


def kernel(
    nsub_ref, nblk_ref, f_hbm, schur_hbm, precond_hbm, modes_hbm, coarse_hbm,
    lam_ref, out_ref,
    fv, mv, stage, khi, klo, shi, slo,
    group, key, source, pick,
    fsend, frecv, mown, msend, mrecv, crows, chi, clo,
    aghi, aglo, kaghi, kaglo, saghi, saglo, ghi, glo,
    wsend, wrecv0, wrecv1, wrecv2, wrecv3, wblk, gath,
    res, kres, zvec, szvec, dirv, qvec, fres,
    hsem, ssem0, rsem0, ssemx, rsemx, ssemg, rsemg,
):
    i, j = lax.axis_index("sub"), lax.axis_index("blk")
    me = i * NBLK_AX + j
    wrecv = (wrecv0, wrecv1, wrecv2, wrecv3)
    yy, xx, zz, cc = i // 4, lax.rem(i, 4), j // 2, lax.rem(j, 2)
    around = [
        (lax.rem(i + 1, NSUB_AX), j),
        (lax.rem(i + NSUB_AX - 1, NSUB_AX), j),
        (i, lax.rem(j + 1, NBLK_AX)),
        (i, lax.rem(j + NBLK_AX - 1, NBLK_AX)),
    ]

    def far(q):
        return 2 + (q * (q + 1)) // 2

    def other(t):
        y = lax.rem(yy + far(t // 32), 4)
        x = lax.rem(xx + far(lax.rem(t // 8, 4)), 4)
        z = lax.rem(zz + far(lax.rem(t // 2, 4)), 4)
        c = lax.rem(cc + 1 + lax.rem(t, 2), 2)
        return (y * 4 + x, z * 2 + c)

    loads = [
        pltpu.make_async_copy(f_hbm, fv, hsem.at[0]),
        pltpu.make_async_copy(modes_hbm, mv, hsem.at[1]),
        pltpu.make_async_copy(coarse_hbm, crows.at[pl.ds(0, 16)], hsem.at[2]),
    ]
    big = [
        pltpu.make_async_copy(mat.at[s], stage.at[2 * n + s], hsem.at[3 + 2 * n + s])
        for n, mat in enumerate((precond_hbm, schur_hbm))
        for s in range(2)
    ]
    for copy in loads + big:
        copy.start()

    barrier = pltpu.get_barrier_semaphore()

    def greet(t, carry):
        pl.semaphore_signal(barrier, inc=1, device_id=other(t), device_id_type=MESH)
        return carry

    lax.fori_loop(0, 127, greet, 0)

    def classify(b, carry):
        s, n = nsub_ref[b // 8, lax.rem(b, 8)], nblk_ref[b // 8, lax.rem(b, 8)]
        dev = s // 2
        dsub, dblk = dev // NBLK_AX, lax.rem(dev, NBLK_AX)
        g = jnp.where(
            dsub == around[0][0], 0,
            jnp.where(dsub == around[1][0], 1, jnp.where(dblk == around[2][1], 2, 3)),
        )
        theirs = lax.rem(s, 2) * 8 + n
        g = jnp.where(s < 0, 4, g)
        group[b] = jnp.where(s < 0, 8, 2 * g + lax.rem(s, 2))
        key[b] = g * 16 + jnp.where((g == 1) | (g == 3), theirs, b)
        return carry

    lax.fori_loop(0, 16, classify, 0)

    def place(b, carry):
        mine = key[b]
        g = mine // 16

        def count(o, slot):
            k = key[o]
            return slot + jnp.where((k < mine) & (k // 16 == g), 1, 0)

        slot = lax.fori_loop(0, 16, count, jnp.int32(0), unroll=True)
        source[b] = jnp.where(g == 4, 16, g * 4 + jnp.minimum(slot, 3))
        return carry

    lax.fori_loop(0, 16, place, 0)

    def invert(t, carry):
        def match(b, found):
            return jnp.where(source[b] == t, b, found)

        pick[t] = lax.fori_loop(0, 16, match, jnp.int32(0), unroll=True)
        return carry

    lax.fori_loop(0, 16, invert, 0)

    for copy in loads:
        copy.wait()

    zero = jnp.zeros((8, 128), F32)
    pad = jnp.zeros((2, 128), F32)
    for b in range(16):
        s, cols = b // 8, slice((b % 8) * 128, (b % 8) * 128 + 128)
        wide = slice(b * 128, b * 128 + 128)
        wblk[b] = fv[s, :, cols]
        m8 = jnp.concatenate([mv[s, :, cols], pad], axis=0)
        mown[b] = m8
        rows = jnp.concatenate([m8, zero] if s == 0 else [zero, m8], axis=0)
        h, l = split(rows)
        ghi[:, wide] = h
        glo[:, wide] = l
        aghi[0:16, wide] = h
        aglo[0:16, wide] = l
    row = lax.broadcasted_iota(jnp.int32, (16, 128), 0)
    ghi[:, 2048:2176] = jnp.where(row == 6, 1.0, 0.0).astype(BF16)
    glo[:, 2048:2176] = jnp.zeros((16, 128), BF16)
    for t in range(16):
        fsend[t] = wblk[pick[t]]
        msend[t] = mown[pick[t]]
    frecv[16] = jnp.zeros((16, 128), F32)
    for buf in wrecv:
        buf[16] = jnp.zeros((16, 128), F32)

    def halve(n, s, hi_ref, lo_ref):
        def step(t, carry):
            rows = pl.ds(pl.multiple_of(t * 32, 32), 32)
            h, l = split(stage[2 * n + s, rows])
            hi_ref[s, rows] = h
            lo_ref[s, rows] = l
            return carry

        big[2 * n + s].wait()
        lax.fori_loop(0, 32, step, 0)

    halve(0, 0, khi, klo)
    halve(0, 1, khi, klo)

    pl.semaphore_wait(barrier, 127)

    first = []
    for g, where in enumerate(around):
        there = g ^ 1
        for n, (src, dst) in enumerate((
            (fsend.at[pl.ds(4 * g, 4)], frecv.at[pl.ds(4 * there, 4)]),
            (msend.at[pl.ds(4 * g, 4)], mrecv.at[pl.ds(4 * there, 4)]),
            (crows.at[pl.ds(0, 16)], crows.at[pl.ds(16 + 16 * there, 16)]),
        )):
            copy = pltpu.make_async_remote_copy(
                src, dst, ssem0.at[3 * g + n], rsem0.at[3 * there + n], where, MESH
            )
            copy.start()
            first.append((n, copy))

    halve(1, 0, shi, slo)

    for n, copy in first:
        if n < 2:
            copy.wait_recv()
    for b in range(16):
        wide = slice(b * 128, b * 128 + 128)
        res[:, wide] = wblk[b] - frecv[source[b]]
        theirs = mrecv[lax.rem(source[b], 16)]
        code = group[b]
        for pair in range(4):
            both = jnp.concatenate(
                [jnp.where(code == 2 * pair + s2, -theirs, 0.0) for s2 in range(2)], axis=0
            )
            h, l = split(both)
            rows = slice(16 + 16 * pair, 32 + 16 * pair)
            aghi[rows, wide] = h
            aglo[rows, wide] = l

    lane = lax.broadcasted_iota(jnp.int32, (16, 128), 1)
    own = (lane // 16) == lax.rem(row, 8)

    def payload(vec, scalar):
        u = jnp.concatenate([vec, scalar], axis=1)
        uh, ul = split(u)
        uh = jnp.concatenate([uh] * 8, axis=0)
        ul = jnp.concatenate([ul] * 8, axis=0)
        both = dot_t(jnp.concatenate([ghi[...], glo[...]], axis=0), uh)
        r = both[:16] + both[16:] + dot_t(ghi[...], ul)
        r = jnp.where(own, r, 0.0)
        return jnp.sum(r.reshape(2, 8, 128), axis=1)

    def spread_out(k, value):
        mine = gath.at[k, me]
        gath[k, me] = value

        def send(t, carry):
            pltpu.make_async_remote_copy(
                mine, mine, ssemg.at[k], rsemg.at[k], other(t), MESH
            ).start()
            return carry

        lax.fori_loop(0, 127, send, 0)

    def wait_all(sem, k):
        many = gath.at[k, pl.ds(0, 127)]
        pltpu.make_async_copy(many, many, sem.at[k]).wait()

    def factors(k):
        wait_all(rsemg, k)
        x = gath.at[k].reshape(256, 128)[...].T
        left = jnp.concatenate([x[16 * m : 16 * m + 16] for m in range(6)], axis=1)
        scalar = jnp.sum(x[96:112], axis=1, keepdims=True)
        return product3(left, chi[...], clo[...], dot_t), scalar

    def apply(hi_ref, lo_ref, s, vec, store):
        for q in range(4):
            cols = slice(q * 256, q * 256 + 256)
            store(
                slice(s * 1024 + q * 256, s * 1024 + q * 256 + 256),
                product3(vec, hi_ref[s, :, cols], lo_ref[s, :, cols]),
            )

    swaps = []

    def swap(k):
        for t in range(16):
            wsend[k, t] = wblk[pick[t]]
        copies = []
        for g, where in enumerate(around):
            there = g ^ 1
            copy = pltpu.make_async_remote_copy(
                wsend.at[k, pl.ds(4 * g, 4)], wrecv[k].at[pl.ds(4 * there, 4)],
                ssemx.at[k, g], rsemx.at[k, there], where, MESH,
            )
            copy.start()
            copies.append(copy)
        for copy in copies:
            copy.wait_recv()
        swaps.extend(copies)

    def assembled(k, b):
        return wblk[b] - wrecv[k][source[b]]

    def block_sum(a, b):
        total = a[:, 0:128] * b[:, 0:128]
        for n in range(1, 16):
            cols = slice(n * 128, n * 128 + 128)
            total = total + a[:, cols] * b[:, cols]
        return total

    def put_blocks(x):
        for b in range(16):
            wblk[b] = x[:, b * 128 : b * 128 + 128]

    spread_out(0, payload(res[...], jnp.zeros((16, 128), F32)))

    halve(1, 1, shi, slo)
    for n, copy in first:
        if n == 2:
            copy.wait_recv()
    h, l = split(crows[...])
    chi[...] = h
    clo[...] = l

    def apply_first(hi_ref, lo_ref, out_hi, out_lo, vec_ref, vec_out):
        for s in range(2):
            cols = slice(s * 1024, s * 1024 + 1024)
            ah, al = aghi[:, cols], aglo[:, cols]
            parts_hi, parts_lo = [ah], [al]
            if vec_ref is not None:
                vh, vl = split(vec_ref[:, cols])
                parts_hi, parts_lo = [vh, ah], [vl, al]
            lh = jnp.concatenate(parts_hi, axis=0)
            ll = jnp.concatenate(parts_lo, axis=0)
            n = lh.shape[0]
            lhl = jnp.concatenate([lh, ll], axis=0)
            for q in range(4):
                c = slice(q * 256, q * 256 + 256)
                o = slice(s * 1024 + q * 256, s * 1024 + q * 256 + 256)
                both = dot(lhl, hi_ref[s, :, c])
                total = both[:n] + both[n:] + dot(lh, lo_ref[s, :, c])
                if vec_ref is not None:
                    vec_out[:, o] = total[:16]
                    total = total[16:]
                oh, ol = split(total)
                out_hi[:, o] = oh
                out_lo[:, o] = ol

    apply_first(khi, klo, kaghi, kaglo, res, kres)
    apply_first(shi, slo, saghi, saglo, None, None)

    fr, _ = factors(0)
    fres[...] = fr
    rho_before = None
    for it in range(ITERS):
        fr = fres[...]
        p = res[...] - product3(fr, aghi[...], aglo[...])
        w = kres[...] - product3(fr, kaghi[...], kaglo[...])
        put_blocks(w)
        part = block_sum(w, p)
        swap(2 * it)
        for b in range(16):
            zvec[:, b * 128 : b * 128 + 128] = assembled(2 * it, b)
        spread_out(1 + 2 * it, payload(zvec[...], part))
        for s in range(2):
            def store(cols, value):
                szvec[:, cols] = value

            apply(shi, slo, s, zvec[:, s * 1024 : s * 1024 + 1024], store)
        fz, rho = factors(1 + 2 * it)
        y = zvec[...] - product3(fz, aghi[...], aglo[...])
        q = szvec[...] - product3(fz, saghi[...], saglo[...])
        if it > 0:
            beta = rho / rho_before
            y = y + beta * dirv[...]
            q = q + beta * qvec[...]
        dirv[...] = y
        qvec[...] = q
        put_blocks(q)
        part = block_sum(q, y)
        swap(2 * it + 1)
        for b in range(16):
            zvec[:, b * 128 : b * 128 + 128] = assembled(2 * it + 1, b)
        spread_out(2 + 2 * it, payload(zvec[...], part))
        if it + 1 < ITERS:
            for s in range(2):
                def store(cols, value):
                    szvec[:, cols] = value

                apply(khi, klo, s, zvec[:, s * 1024 : s * 1024 + 1024], store)
        fi, sigma = factors(2 + 2 * it)
        step = rho / sigma
        for s in range(2):
            cols = slice(s * 1024, s * 1024 + 1024)
            add = step * dirv[:, cols]
            if it == 0:
                lam_ref[s] = add
            else:
                lam_ref[s] += add
        res[...] = res[...] - step * zvec[...]
        if it + 1 < ITERS:
            kres[...] = kres[...] - step * szvec[...]
        fres[...] = fres[...] - step * fi
        rho_before = rho

    p = res[...] - product3(fres[...], aghi[...], aglo[...])
    for s in range(2):
        out_ref[s] = p[:, s * 1024 : s * 1024 + 1024]

    for _, copy in first:
        copy.wait_send()
    for copy in swaps:
        copy.wait_send()
    for k in range(GATHERS):
        wait_all(ssemg, k)


def per_device(f_local, schur, precond, modes, coarse_inv, nbr_sub, nbr_blk):
    rows = coarse_inv.reshape(2, 6, 256, 6).transpose(0, 1, 3, 2).reshape(2, 6, 1536)
    rows = jnp.pad(rows, ((0, 0), (0, 2), (0, 0))).reshape(16, 1536)
    dma = pltpu.SemaphoreType.DMA
    vec = pltpu.VMEM((16, 2048), F32)
    out = jax.ShapeDtypeStruct((2, 16, 1024), F32)
    anywhere = pl.BlockSpec(memory_space=pl.ANY)
    smem = pl.BlockSpec(memory_space=pltpu.SMEM)
    half = pltpu.VMEM((2, 1024, 1024), BF16)
    tall = pltpu.VMEM((ROWS, 2048), BF16)
    blocks = pltpu.VMEM((17, 16, 128), F32)
    table = pltpu.SMEM((16,), jnp.int32)
    return pl.pallas_call(
        kernel,
        out_shape=(out, out),
        in_specs=[smem, smem] + [anywhere] * 5,
        out_specs=(pl.BlockSpec(memory_space=pltpu.VMEM),) * 2,
        scratch_shapes=[
            pltpu.VMEM((2, 16, 1024), F32), pltpu.VMEM((2, 6, 1024), F32),
            pltpu.VMEM((4, 1024, 1024), F32), half, half, half, half,
            table, table, table, table,
            pltpu.VMEM((16, 16, 128), F32), pltpu.VMEM((17, 16, 128), F32),
            pltpu.VMEM((16, 8, 128), F32), pltpu.VMEM((16, 8, 128), F32), pltpu.VMEM((16, 8, 128), F32),
            pltpu.VMEM((ROWS, 1536), F32),
            pltpu.VMEM((ROWS, 1536), BF16), pltpu.VMEM((ROWS, 1536), BF16),
            tall, tall, tall, tall, tall, tall,
            pltpu.VMEM((16, 2176), BF16), pltpu.VMEM((16, 2176), BF16),
            pltpu.VMEM((SWAPS, 16, 16, 128), F32), blocks, blocks, blocks, blocks,
            pltpu.VMEM((16, 16, 128), F32),
            pltpu.VMEM((GATHERS, 128, 2, 128), F32),
            vec, vec, vec, vec, vec, vec,
            pltpu.VMEM((16, ROWS), F32),
            dma((7,)), dma((12,)), dma((12,)), dma((SWAPS, 4)), dma((SWAPS, 4)),
            dma((GATHERS,)), dma((GATHERS,)),
        ],
        compiler_params=pltpu.CompilerParams(
            collective_id=0, has_side_effects=True, vmem_limit_bytes=56 * 2**20
        ),
        cost_estimate=pl.CostEstimate(flops=10**9, bytes_accessed=2 * 10**7, transcendentals=0),
    )(nbr_sub, nbr_blk, f_local, schur, precond, modes, rows)


def solution(mesh):
    flat = P(("sub", "blk"), None)
    tall = P(("sub", "blk"), None, None)
    return jax.shard_map(
        per_device,
        mesh=mesh,
        in_specs=(tall, tall, tall, tall, flat, flat, flat),
        out_specs=(tall, tall),
        check_vma=False,
    )
```

```python
import jax
import jax.numpy as jnp
from jax import lax
from jax.experimental import pallas as pl
from jax.experimental.pallas import tpu as pltpu
from jax.sharding import PartitionSpec as P

ITERS = 2
GATHERS = 1 + 2 * ITERS
SWAPS = 2 * ITERS
NSUB_AX, NBLK_AX = 16, 8
ROWS = 80
MESH = pl.DeviceIdType.MESH
F32, BF16 = jnp.float32, jnp.bfloat16


def split(x):
    hi = x.astype(BF16)
    return hi, (x - hi.astype(F32)).astype(BF16)


def dot(a, b):
    return jnp.dot(a, b, preferred_element_type=F32)


def dot_t(a, b):
    return lax.dot_general(a, b, (((1,), (1,)), ((), ())), preferred_element_type=F32)


def product3(x, hi, lo, mul=dot):
    rows = x.shape[0]
    xh, xl = split(x)
    both = mul(jnp.concatenate([xh, xl], axis=0), hi)
    return both[:rows] + both[rows:] + mul(xh, lo)


def kernel(
    nsub_ref, nblk_ref, f_hbm, schur_hbm, precond_hbm, modes_hbm, coarse_hbm,
    lam_ref, out_ref,
    fv, mv, craw, cpad, order, stage, khi, klo, shi, slo,
    group, key, source, pick,
    fsend, frecv, mown, msend, mrecv, crows, cboth,
    aghi, aglo, kaghi, kaglo, saghi, saglo, ghi, glo,
    wsend, wrecv0, wrecv1, wrecv2, wrecv3, wblk, gath,
    res, kres, zvec, szvec, dirv, qvec, fres,
    hsem, ssem0, rsem0, ssemx, rsemx, ssemg, rsemg,
):
    i, j = lax.axis_index("sub"), lax.axis_index("blk")
    me = i * NBLK_AX + j
    wrecv = (wrecv0, wrecv1, wrecv2, wrecv3)
    yy, xx, zz, cc = i // 4, lax.rem(i, 4), j // 2, lax.rem(j, 2)
    around = [
        (lax.rem(i + 1, NSUB_AX), j),
        (lax.rem(i + NSUB_AX - 1, NSUB_AX), j),
        (i, lax.rem(j + 1, NBLK_AX)),
        (i, lax.rem(j + NBLK_AX - 1, NBLK_AX)),
    ]

    def far(q):
        return 2 + (q * (q + 1)) // 2

    columns = [
        lax.rem(zz + dz, 4) * 2 + lax.rem(cc + dc, 2) for dz in (2, 1, 3, 0) for dc in (1, 0)
    ]

    def each_other(act):
        def row(t, carry):
            y = lax.rem(yy + far(t // 4), 4)
            x = lax.rem(xx + far(lax.rem(t, 4)), 4)
            for column in columns:
                act((y * 4 + x, column))
            return carry

        lax.fori_loop(0, 15, row, 0)
        for column in columns[:-1]:
            act((i, column))

    loads = [
        pltpu.make_async_copy(f_hbm, fv, hsem.at[0]),
        pltpu.make_async_copy(modes_hbm, mv, hsem.at[1]),
        pltpu.make_async_copy(coarse_hbm, craw, hsem.at[2]),
    ]
    big = [
        pltpu.make_async_copy(mat.at[s], stage.at[2 * n + s], hsem.at[3 + 2 * n + s])
        for n, mat in enumerate((precond_hbm, schur_hbm))
        for s in range(2)
    ]
    for copy in loads + big:
        copy.start()

    barrier = pltpu.get_barrier_semaphore()

    each_other(
        lambda where: pl.semaphore_signal(barrier, inc=1, device_id=where, device_id_type=MESH)
    )

    def classify(b, carry):
        s, n = nsub_ref[b // 8, lax.rem(b, 8)], nblk_ref[b // 8, lax.rem(b, 8)]
        dev = s // 2
        dsub, dblk = dev // NBLK_AX, lax.rem(dev, NBLK_AX)
        g = jnp.where(
            dsub == around[0][0], 0,
            jnp.where(dsub == around[1][0], 1, jnp.where(dblk == around[2][1], 2, 3)),
        )
        theirs = lax.rem(s, 2) * 8 + n
        g = jnp.where(s < 0, 4, g)
        group[b] = jnp.where(s < 0, 8, 2 * g + lax.rem(s, 2))
        key[b] = g * 16 + jnp.where((g == 1) | (g == 3), theirs, b)
        return carry

    lax.fori_loop(0, 16, classify, 0)

    def place(b, carry):
        mine = key[b]
        g = mine // 16

        def count(o, slot):
            k = key[o]
            return slot + jnp.where((k < mine) & (k // 16 == g), 1, 0)

        slot = lax.fori_loop(0, 16, count, jnp.int32(0), unroll=True)
        source[b] = jnp.where(g == 4, 16, g * 4 + jnp.minimum(slot, 3))
        return carry

    lax.fori_loop(0, 16, place, 0)

    def invert(t, carry):
        def match(b, found):
            return jnp.where(source[b] == t, b, found)

        pick[t] = lax.fori_loop(0, 16, match, jnp.int32(0), unroll=True)
        return carry

    lax.fori_loop(0, 16, invert, 0)

    for copy in loads:
        copy.wait()

    zero = jnp.zeros((8, 128), F32)
    pad = jnp.zeros((2, 128), F32)
    for b in range(16):
        s, cols = b // 8, slice((b % 8) * 128, (b % 8) * 128 + 128)
        wide = slice(b * 128, b * 128 + 128)
        wblk[b] = fv[s, :, cols]
        m8 = jnp.concatenate([mv[:, s, cols], pad], axis=0)
        mown[b] = m8
        rows = jnp.concatenate([m8, zero] if s == 0 else [zero, m8], axis=0)
        h, l = split(rows)
        ghi[:, wide] = h
        glo[:, wide] = l
        aghi[0:16, wide] = h
        aglo[0:16, wide] = l
    col = lax.broadcasted_iota(jnp.int32, (1, 768), 1)
    wanted = 6 * lax.rem(col, 128) + col // 128
    for n in range(6):
        rows = slice(n * 128, n * 128 + 128)
        here = lax.broadcasted_iota(jnp.int32, (128, 768), 0) + n * 128
        order[rows] = jnp.where(here == wanted, 1.0, 0.0).astype(BF16)
    cpad[...] = jnp.zeros((16, 1536), F32)
    cpad[0:6] = craw[0:6]
    cpad[8:14] = craw[6:12]
    for h in range(2):
        cols = slice(768 * h, 768 * h + 768)
        ch, cl = split(cpad[:, cols])
        both = dot(jnp.concatenate([ch, cl], axis=0), order[...])
        crows[0:16, cols] = both[:16] + both[16:]
    row = lax.broadcasted_iota(jnp.int32, (16, 128), 0)
    ghi[:, 2048:2176] = jnp.where(row == 6, 1.0, 0.0).astype(BF16)
    glo[:, 2048:2176] = jnp.zeros((16, 128), BF16)
    for t in range(16):
        fsend[t] = wblk[pick[t]]
        msend[t] = mown[pick[t]]
    crows[ROWS:128] = jnp.zeros((128 - ROWS, 1536), F32)
    frecv[16] = jnp.zeros((16, 128), F32)
    for buf in wrecv:
        buf[16] = jnp.zeros((16, 128), F32)

    def halve(n, s, hi_ref, lo_ref):
        def step(t, carry):
            rows = pl.ds(pl.multiple_of(t * 64, 64), 64)
            h, l = split(stage[2 * n + s, rows])
            hi_ref[s, rows] = h
            lo_ref[s, rows] = l
            return carry

        big[2 * n + s].wait()
        lax.fori_loop(0, 16, step, 0, unroll=2)

    halve(0, 0, khi, klo)
    halve(0, 1, khi, klo)

    pl.semaphore_wait(barrier, 127)

    first = []
    for g, where in enumerate(around):
        there = g ^ 1
        for n, (src, dst) in enumerate((
            (fsend.at[pl.ds(4 * g, 4)], frecv.at[pl.ds(4 * there, 4)]),
            (msend.at[pl.ds(4 * g, 4)], mrecv.at[pl.ds(4 * there, 4)]),
            (crows.at[pl.ds(0, 16)], crows.at[pl.ds(16 + 16 * there, 16)]),
        )):
            copy = pltpu.make_async_remote_copy(
                src, dst, ssem0.at[3 * g + n], rsem0.at[3 * there + n], where, MESH
            )
            copy.start()
            first.append((n, copy))

    halve(1, 0, shi, slo)

    for n, copy in first:
        if n < 2:
            copy.wait_recv()
    for b in range(16):
        wide = slice(b * 128, b * 128 + 128)
        res[:, wide] = wblk[b] - frecv[source[b]]
        theirs = mrecv[lax.rem(source[b], 16)]
        code = group[b]
        for pair in range(4):
            both = jnp.concatenate(
                [jnp.where(code == 2 * pair + s2, -theirs, 0.0) for s2 in range(2)], axis=0
            )
            h, l = split(both)
            rows = slice(16 + 16 * pair, 32 + 16 * pair)
            aghi[rows, wide] = h
            aglo[rows, wide] = l

    lane = lax.broadcasted_iota(jnp.int32, (16, 128), 1)
    own = (lane // 16) == lax.rem(row, 8)

    def payload(vec, scalar):
        u = jnp.concatenate([vec, scalar], axis=1)
        uh, ul = split(u)
        uh = jnp.concatenate([uh] * 8, axis=0)
        ul = jnp.concatenate([ul] * 8, axis=0)
        both = dot_t(jnp.concatenate([ghi[...], glo[...]], axis=0), uh)
        r = both[:16] + both[16:] + dot_t(ghi[...], ul)
        r = jnp.where(own, r, 0.0)
        return jnp.sum(r.reshape(2, 8, 128), axis=1)

    def spread_out(k, value):
        mine = gath.at[k, me]
        gath[k, me] = value

        each_other(
            lambda where: pltpu.make_async_remote_copy(
                mine, mine, ssemg.at[k], rsemg.at[k], where, MESH
            ).start()
        )

    def wait_all(sem, k):
        many = gath.at[k, pl.ds(0, 127)]
        pltpu.make_async_copy(many, many, sem.at[k]).wait()

    def factors(k):
        wait_all(rsemg, k)
        x = gath.at[k].reshape(256, 128)[...].T
        scalar = jnp.sum(x[96:112], axis=1, keepdims=True)
        left = jnp.concatenate(
            [
                jnp.concatenate(
                    [part[16 * m : 16 * m + 16, 128 * h : 128 * h + 128] for h in range(2) for m in range(6)],
                    axis=1,
                )
                for part in split(x)
            ],
            axis=0,
        )
        both = dot(left, cboth[...])
        return (both[:16, :128] + both[16:, :128] + both[:16, 128:])[:, :ROWS], scalar

    def apply(hi_ref, lo_ref, s, vec, store):
        for q in range(4):
            cols = slice(q * 256, q * 256 + 256)
            store(
                slice(s * 1024 + q * 256, s * 1024 + q * 256 + 256),
                product3(vec, hi_ref[s, :, cols], lo_ref[s, :, cols]),
            )

    swaps = []

    def swap(k):
        for t in range(16):
            wsend[k, t] = wblk[pick[t]]
        copies = []
        for g, where in enumerate(around):
            there = g ^ 1
            copy = pltpu.make_async_remote_copy(
                wsend.at[k, pl.ds(4 * g, 4)], wrecv[k].at[pl.ds(4 * there, 4)],
                ssemx.at[k, g], rsemx.at[k, there], where, MESH,
            )
            copy.start()
            copies.append(copy)
        for copy in copies:
            copy.wait_recv()
        swaps.extend(copies)

    def assembled(k, b):
        return wblk[b] - wrecv[k][source[b]]

    def block_sum(a, b):
        total = a[:, 0:128] * b[:, 0:128]
        for n in range(1, 16):
            cols = slice(n * 128, n * 128 + 128)
            total = total + a[:, cols] * b[:, cols]
        return total

    def put_blocks(x):
        for b in range(16):
            wblk[b] = x[:, b * 128 : b * 128 + 128]

    spread_out(0, payload(res[...], jnp.zeros((16, 128), F32)))

    halve(1, 1, shi, slo)
    for n, copy in first:
        if n == 2:
            copy.wait_recv()
    h, l = split(crows[...].T)
    cboth[:, 0:128] = h
    cboth[:, 128:256] = l

    def apply_first(hi_ref, lo_ref, out_hi, out_lo, vec_ref, vec_out):
        for s in range(2):
            cols = slice(s * 1024, s * 1024 + 1024)
            ah, al = aghi[:, cols], aglo[:, cols]
            parts_hi, parts_lo = [ah], [al]
            if vec_ref is not None:
                vh, vl = split(vec_ref[:, cols])
                parts_hi, parts_lo = [vh, ah], [vl, al]
            lh = jnp.concatenate(parts_hi, axis=0)
            ll = jnp.concatenate(parts_lo, axis=0)
            n = lh.shape[0]
            lhl = jnp.concatenate([lh, ll], axis=0)
            for q in range(4):
                c = slice(q * 256, q * 256 + 256)
                o = slice(s * 1024 + q * 256, s * 1024 + q * 256 + 256)
                both = dot(lhl, hi_ref[s, :, c])
                total = both[:n] + both[n:] + dot(lh, lo_ref[s, :, c])
                if vec_ref is not None:
                    vec_out[:, o] = total[:16]
                    total = total[16:]
                oh, ol = split(total)
                out_hi[:, o] = oh
                out_lo[:, o] = ol

    apply_first(khi, klo, kaghi, kaglo, res, kres)
    apply_first(shi, slo, saghi, saglo, None, None)

    fr, _ = factors(0)
    fres[...] = fr
    rho_before = None
    for it in range(ITERS):
        fr = fres[...]
        p = res[...] - product3(fr, aghi[...], aglo[...])
        w = kres[...] - product3(fr, kaghi[...], kaglo[...])
        put_blocks(w)
        part = block_sum(w, p)
        swap(2 * it)
        for b in range(16):
            zvec[:, b * 128 : b * 128 + 128] = assembled(2 * it, b)
        spread_out(1 + 2 * it, payload(zvec[...], part))
        for s in range(2):
            def store(cols, value):
                szvec[:, cols] = value

            apply(shi, slo, s, zvec[:, s * 1024 : s * 1024 + 1024], store)
        fz, rho = factors(1 + 2 * it)
        y = zvec[...] - product3(fz, aghi[...], aglo[...])
        q = szvec[...] - product3(fz, saghi[...], saglo[...])
        if it > 0:
            beta = rho / rho_before
            y = y + beta * dirv[...]
            q = q + beta * qvec[...]
        dirv[...] = y
        qvec[...] = q
        put_blocks(q)
        part = block_sum(q, y)
        swap(2 * it + 1)
        for b in range(16):
            zvec[:, b * 128 : b * 128 + 128] = assembled(2 * it + 1, b)
        spread_out(2 + 2 * it, payload(zvec[...], part))
        if it + 1 < ITERS:
            for s in range(2):
                def store(cols, value):
                    szvec[:, cols] = value

                apply(khi, klo, s, zvec[:, s * 1024 : s * 1024 + 1024], store)
        fi, sigma = factors(2 + 2 * it)
        step = rho / sigma
        for s in range(2):
            cols = slice(s * 1024, s * 1024 + 1024)
            add = step * dirv[:, cols]
            if it == 0:
                lam_ref[s] = add
            else:
                lam_ref[s] += add
        res[...] = res[...] - step * zvec[...]
        if it + 1 < ITERS:
            kres[...] = kres[...] - step * szvec[...]
        fres[...] = fres[...] - step * fi
        rho_before = rho

    p = res[...] - product3(fres[...], aghi[...], aglo[...])
    for s in range(2):
        out_ref[s] = p[:, s * 1024 : s * 1024 + 1024]

    for _, copy in first:
        copy.wait_send()
    for copy in swaps:
        copy.wait_send()
    for k in range(GATHERS):
        wait_all(ssemg, k)


def per_device(f_local, schur, precond, modes, coarse_inv, nbr_sub, nbr_blk):
    dma = pltpu.SemaphoreType.DMA
    vec = pltpu.VMEM((16, 2048), F32)
    out = jax.ShapeDtypeStruct((2, 16, 1024), F32)
    anywhere = pl.BlockSpec(memory_space=pl.ANY)
    smem = pl.BlockSpec(memory_space=pltpu.SMEM)
    half = pltpu.VMEM((2, 1024, 1024), BF16)
    tall = pltpu.VMEM((ROWS, 2048), BF16)
    blocks = pltpu.VMEM((17, 16, 128), F32)
    table = pltpu.SMEM((16,), jnp.int32)
    return pl.pallas_call(
        kernel,
        out_shape=(out, out),
        in_specs=[smem, smem] + [anywhere] * 5,
        out_specs=(pl.BlockSpec(memory_space=pltpu.VMEM),) * 2,
        scratch_shapes=[
            pltpu.VMEM((2, 16, 1024), F32), pltpu.VMEM((6, 2, 1024), F32),
            pltpu.VMEM((12, 1536), F32), pltpu.VMEM((16, 1536), F32), pltpu.VMEM((768, 768), BF16),
            pltpu.VMEM((4, 1024, 1024), F32), half, half, half, half,
            table, table, table, table,
            pltpu.VMEM((16, 16, 128), F32), pltpu.VMEM((17, 16, 128), F32),
            pltpu.VMEM((16, 8, 128), F32), pltpu.VMEM((16, 8, 128), F32), pltpu.VMEM((16, 8, 128), F32),
            pltpu.VMEM((128, 1536), F32), pltpu.VMEM((1536, 256), BF16),
            tall, tall, tall, tall, tall, tall,
            pltpu.VMEM((16, 2176), BF16), pltpu.VMEM((16, 2176), BF16),
            pltpu.VMEM((SWAPS, 16, 16, 128), F32), blocks, blocks, blocks, blocks,
            pltpu.VMEM((16, 16, 128), F32),
            pltpu.VMEM((GATHERS, 128, 2, 128), F32),
            vec, vec, vec, vec, vec, vec,
            pltpu.VMEM((16, ROWS), F32),
            dma((7,)), dma((12,)), dma((12,)), dma((SWAPS, 4)), dma((SWAPS, 4)),
            dma((GATHERS,)), dma((GATHERS,)),
        ],
        compiler_params=pltpu.CompilerParams(
            collective_id=0, has_side_effects=True, vmem_limit_bytes=56 * 2**20
        ),
        cost_estimate=pl.CostEstimate(flops=10**9, bytes_accessed=2 * 10**7, transcendentals=0),
    )(nbr_sub, nbr_blk, f_local, schur, precond, modes.transpose(1, 0, 2), coarse_inv)


def solution(mesh):
    flat = P(("sub", "blk"), None)
    tall = P(("sub", "blk"), None, None)
    return jax.shard_map(
        per_device,
        mesh=mesh,
        in_specs=(tall, tall, tall, tall, flat, flat, flat),
        out_specs=(tall, tall),
        check_vma=False,
    )
```

```python
import jax
import jax.numpy as jnp
from jax import lax
from jax.experimental import pallas as pl
from jax.experimental.pallas import tpu as pltpu
from jax.sharding import PartitionSpec as P

ITERS = 2
GATHERS = 1 + 2 * ITERS
SWAPS = 2 * ITERS
NSUB_AX, NBLK_AX = 16, 8
ROWS = 80
BACK = (1, 0, 2, 3)
MESH = pl.DeviceIdType.MESH
F32, BF16 = jnp.float32, jnp.bfloat16


def split(x):
    hi = x.astype(BF16)
    return hi, (x - hi.astype(F32)).astype(BF16)


def dot(a, b):
    return jnp.dot(a, b, preferred_element_type=F32)


def dot_t(a, b):
    return lax.dot_general(a, b, (((1,), (1,)), ((), ())), preferred_element_type=F32)


def product3(x, hi, lo, mul=dot):
    rows = x.shape[0]
    xh, xl = split(x)
    both = mul(jnp.concatenate([xh, xl], axis=0), hi)
    return both[:rows] + both[rows:] + mul(xh, lo)


def kernel(
    nsub_ref, nblk_ref, f_hbm, schur_hbm, precond_hbm, modes_hbm, coarse_hbm,
    lam_ref, out_ref,
    fv, mv, craw, cpad, order, stage, khi, klo, shi, slo,
    group, key, source, pick,
    fsend, frecv, mown, msend, mrecv, crows, cboth,
    aghi, aglo, kaghi, kaglo, saghi, saglo,
    wsend, wrecv0, wrecv1, wrecv2, wrecv3, wblk, gath, fpart, fmate,
    res, kres, zvec, szvec, dirv, qvec, fres,
    hsem, ssem0, rsem0, ssemx, rsemx, ssemg, rsemg, ssemf, rsemf,
):
    i, j = lax.axis_index("sub"), lax.axis_index("blk")
    wrecv = (wrecv0, wrecv1, wrecv2, wrecv3)
    yy, xx, zz, cc = i // 4, lax.rem(i, 4), j // 2, lax.rem(j, 2)
    around = [
        (lax.rem(i + 1, NSUB_AX), j),
        (lax.rem(i + NSUB_AX - 1, NSUB_AX), j),
        (i, lax.rem(j + NBLK_AX - 1 + 2 * cc, NBLK_AX)),
        (i, j + 1 - 2 * cc),
    ]
    slot = i * 4 + zz

    def far(q):
        return 2 + (q * (q + 1)) // 2

    columns = [lax.rem(zz + dz, 4) * 2 + cc for dz in (2, 1, 3, 0)]

    def each_chip(act):
        def row(t, carry):
            y = lax.rem(yy + far(t // 4), 4)
            x = lax.rem(xx + far(lax.rem(t, 4)), 4)
            for column in columns:
                act((y * 4 + x, column))
            return carry

        lax.fori_loop(0, 15, row, 0)
        for column in columns[:-1]:
            act((i, column))

    loads = [
        pltpu.make_async_copy(f_hbm, fv, hsem.at[0]),
        pltpu.make_async_copy(modes_hbm, mv, hsem.at[1]),
        pltpu.make_async_copy(coarse_hbm, craw, hsem.at[2]),
    ]
    big = [
        pltpu.make_async_copy(mat.at[s], stage.at[2 * n + s], hsem.at[3 + 2 * n + s])
        for n, mat in enumerate((precond_hbm, schur_hbm))
        for s in range(2)
    ]
    for copy in loads + big:
        copy.start()

    barrier = pltpu.get_barrier_semaphore()

    def greet(where):
        pl.semaphore_signal(barrier, inc=1, device_id=where, device_id_type=MESH)

    each_chip(greet)
    greet(around[2])
    greet(around[3])

    def classify(b, carry):
        s, n = nsub_ref[b // 8, lax.rem(b, 8)], nblk_ref[b // 8, lax.rem(b, 8)]
        dev = s // 2
        dsub, dblk = dev // NBLK_AX, lax.rem(dev, NBLK_AX)
        g = jnp.where(
            dsub == around[0][0], 0,
            jnp.where(dsub == around[1][0], 1, jnp.where(dblk == around[2][1], 2, 3)),
        )
        theirs = lax.rem(s, 2) * 8 + n
        g = jnp.where(s < 0, 4, g)
        group[b] = jnp.where(s < 0, 8, 2 * g + lax.rem(s, 2))
        mine = (g == 0) | (g == 4) | ((g >= 2) & (cc == 0))
        key[b] = g * 16 + jnp.where(mine, b, theirs)
        return carry

    lax.fori_loop(0, 16, classify, 0)

    def rank(b, carry):
        mine = key[b]
        g = mine // 16

        def count(o, slot):
            k = key[o]
            return slot + jnp.where((k < mine) & (k // 16 == g), 1, 0)

        slot = lax.fori_loop(0, 16, count, jnp.int32(0), unroll=True)
        source[b] = jnp.where(g == 4, 16, g * 4 + jnp.minimum(slot, 3))
        return carry

    lax.fori_loop(0, 16, rank, 0)

    def invert(t, carry):
        def match(b, found):
            return jnp.where(source[b] == t, b, found)

        pick[t] = lax.fori_loop(0, 16, match, jnp.int32(0), unroll=True)
        return carry

    lax.fori_loop(0, 16, invert, 0)

    for copy in loads:
        copy.wait()

    zero = jnp.zeros((8, 128), F32)
    pad = jnp.zeros((2, 128), F32)
    for b in range(16):
        s, cols = b // 8, slice((b % 8) * 128, (b % 8) * 128 + 128)
        wide = slice(b * 128, b * 128 + 128)
        wblk[b] = fv[s, :, cols]
        m8 = jnp.concatenate([mv[:, s, cols], pad], axis=0)
        mown[b] = m8
        rows = jnp.concatenate([m8, zero] if s == 0 else [zero, m8], axis=0)
        h, l = split(rows)
        aghi[0:16, wide] = h
        aglo[0:16, wide] = l
    col = lax.broadcasted_iota(jnp.int32, (1, 768), 1)
    spot = lax.rem(col, 128)
    wanted = 16 * lax.rem(spot // 8, 8) + 4 * lax.rem(spot // 2, 4) + 2 * (spot // 64)
    wanted = 6 * (wanted + lax.rem(spot, 2)) + col // 128
    for n in range(6):
        rows = slice(n * 128, n * 128 + 128)
        here = lax.broadcasted_iota(jnp.int32, (128, 768), 0) + n * 128
        order[rows] = jnp.where(here == wanted, 1.0, 0.0).astype(BF16)
    cpad[...] = jnp.zeros((16, 1536), F32)
    cpad[0:6] = craw[0:6]
    cpad[8:14] = craw[6:12]
    for h in range(2):
        cols = slice(768 * h, 768 * h + 768)
        ch, cl = split(cpad[:, cols])
        both = dot(jnp.concatenate([ch, cl], axis=0), order[...])
        crows[0:16, cols] = both[:16] + both[16:]
    row = lax.broadcasted_iota(jnp.int32, (ROWS, 128), 0)
    aghi[:, 2048:2176] = jnp.where(row == 6, 1.0, 0.0).astype(BF16)
    aglo[:, 2048:2176] = jnp.zeros((ROWS, 128), BF16)
    for t in range(16):
        fsend[t] = wblk[pick[t]]
        msend[t] = mown[pick[t]]
    frecv[16] = jnp.zeros((16, 128), F32)
    for buf in wrecv:
        buf[16] = jnp.zeros((16, 128), F32)

    def halve(n, s, hi_ref, lo_ref):
        def step(t, carry):
            rows = pl.ds(pl.multiple_of(t * 64, 64), 64)
            h, l = split(stage[2 * n + s, rows])
            hi_ref[s, rows] = h
            lo_ref[s, rows] = l
            return carry

        big[2 * n + s].wait()
        lax.fori_loop(0, 16, step, 0, unroll=2)

    pl.semaphore_wait(barrier, 65)

    first = [[], [], []]
    sources = ((msend, mrecv, 4), (fsend, frecv, 4), (crows, crows, 16))

    def start_first(n):
        src, dst, size = sources[n]
        for g, where in enumerate(around):
            there = BACK[g]
            if n < 2:
                a, b = src.at[pl.ds(size * g, size)], dst.at[pl.ds(size * there, size)]
            else:
                a, b = src.at[pl.ds(0, 16)], dst.at[pl.ds(16 + 16 * there, 16)]
            copy = pltpu.make_async_remote_copy(
                a, b, ssem0.at[4 * n + g], rsem0.at[4 * n + there], where, MESH
            )
            copy.start()
            first[n].append(copy)

    start_first(0)
    halve(0, 0, khi, klo)
    start_first(1)
    start_first(2)
    halve(0, 1, khi, klo)
    for copy in first[0]:
        copy.wait_recv()
    for b in range(16):
        wide = slice(b * 128, b * 128 + 128)
        theirs = mrecv[lax.rem(source[b], 16)]
        code = group[b]
        for pair in range(4):
            both = jnp.concatenate(
                [jnp.where(code == 2 * pair + s2, -theirs, 0.0) for s2 in range(2)], axis=0
            )
            h, l = split(both)
            rows = slice(16 + 16 * pair, 32 + 16 * pair)
            aghi[rows, wide] = h
            aglo[rows, wide] = l

    lane = lax.broadcasted_iota(jnp.int32, (ROWS, 128), 1)
    own = (lane // 16) == lax.rem(row, 8)

    def payload(vec, scalar):
        u = jnp.concatenate([vec, scalar], axis=1)
        uh, ul = split(u)
        uh = jnp.concatenate([uh] * 8, axis=0)
        ul = jnp.concatenate([ul] * 8, axis=0)
        both = dot_t(jnp.concatenate([aghi[...], aglo[...]], axis=0), uh)
        r = both[:ROWS] + both[ROWS:] + dot_t(aghi[...], ul)
        r = jnp.where(own, r, 0.0)
        return jnp.sum(r.reshape(5, 2, 8, 128), axis=2)

    def spread_out(k, value):
        mine = gath.at[k, :, slot]
        gath[k, :, slot] = value
        each_chip(
            lambda where: pltpu.make_async_remote_copy(
                mine, mine, ssemg.at[k], rsemg.at[k], where, MESH
            ).start()
        )

    def wait_all(sem, k):
        many = gath.at[k, :, pl.ds(0, 63)]
        pltpu.make_async_copy(many, many, sem.at[k]).wait()

    mates = []

    def factors(k):
        wait_all(rsemg, k)
        mine, plus, minus, along, mate = [gath.at[k, n].reshape(128, 128)[...] for n in range(5)]
        same = mine + jnp.concatenate([plus[120:], plus[:120]], axis=0)
        same = same + jnp.concatenate([minus[8:], minus[:8]], axis=0)
        place = lax.rem(lax.broadcasted_iota(jnp.int32, (128, 128), 0), 8)
        up = jnp.where(place < 6, pltpu.roll(along, 126, 0), pltpu.roll(along, 6, 0))
        down = jnp.where(place >= 2, pltpu.roll(along, 2, 0), pltpu.roll(along, 122, 0))
        other = mate + jnp.where(cc == 0, up, down)
        first_core = jnp.where(cc == 0, same, other)
        last_core = jnp.where(cc == 0, other, same)
        x = jnp.concatenate(
            [first_core[:64], last_core[:64], first_core[64:], last_core[64:]], axis=0
        ).T
        scalar = jnp.sum(x[96:112], axis=1, keepdims=True)
        left = jnp.concatenate(
            [
                jnp.concatenate(
                    [part[16 * m : 16 * m + 16, 128 * h : 128 * h + 128] for h in range(2) for m in range(6)],
                    axis=1,
                )
                for part in split(x)
            ],
            axis=0,
        )
        both = dot(left, cboth[...])
        part = both[:16, :128] + both[16:, :128] + both[:16, 128:]
        part = jnp.where(lane[:16] == 6, scalar, part)
        fpart[k] = part
        copy = pltpu.make_async_remote_copy(
            fpart.at[k], fmate.at[k], ssemf.at[k], rsemf.at[k], around[3], MESH
        )
        copy.start()
        mates.append(copy)
        copy.wait_recv()
        mates_part = fmate[k]
        total = part + pltpu.roll(mates_part, 64, 1)
        return total[:, :ROWS], part[:, 6:7] + mates_part[:, 6:7]

    def apply(hi_ref, lo_ref, s, vec, store):
        for q in range(4):
            cols = slice(q * 256, q * 256 + 256)
            store(
                slice(s * 1024 + q * 256, s * 1024 + q * 256 + 256),
                product3(vec, hi_ref[s, :, cols], lo_ref[s, :, cols]),
            )

    swaps = []

    def swap(k):
        for t in range(16):
            wsend[k, t] = wblk[pick[t]]
        copies = []
        for g, where in enumerate(around):
            there = BACK[g]
            copy = pltpu.make_async_remote_copy(
                wsend.at[k, pl.ds(4 * g, 4)], wrecv[k].at[pl.ds(4 * there, 4)],
                ssemx.at[k, g], rsemx.at[k, there], where, MESH,
            )
            copy.start()
            copies.append(copy)
        swaps.extend(copies)
        return copies

    def assembled(k, b):
        return wblk[b] - wrecv[k][source[b]]

    def block_sum(a, b):
        total = a[:, 0:128] * b[:, 0:128]
        for n in range(1, 16):
            cols = slice(n * 128, n * 128 + 128)
            total = total + a[:, cols] * b[:, cols]
        return total

    def put_blocks(x):
        for b in range(16):
            wblk[b] = x[:, b * 128 : b * 128 + 128]

    spread_out(0, payload(jnp.concatenate([wblk[b] for b in range(16)], axis=1), jnp.zeros((16, 128), F32)))
    for copy in first[1]:
        copy.wait_recv()
    for b in range(16):
        res[:, b * 128 : b * 128 + 128] = wblk[b] - frecv[source[b]]

    def apply_first(hi_ref, lo_ref, out_hi, out_lo, vec_ref, vec_out):
        for s in range(2):
            cols = slice(s * 1024, s * 1024 + 1024)
            ah, al = aghi[:, cols], aglo[:, cols]
            parts_hi, parts_lo = [ah], [al]
            if vec_ref is not None:
                vh, vl = split(vec_ref[:, cols])
                parts_hi, parts_lo = [vh, ah], [vl, al]
            lh = jnp.concatenate(parts_hi, axis=0)
            ll = jnp.concatenate(parts_lo, axis=0)
            n = lh.shape[0]
            lhl = jnp.concatenate([lh, ll], axis=0)
            for q in range(4):
                c = slice(q * 256, q * 256 + 256)
                o = slice(s * 1024 + q * 256, s * 1024 + q * 256 + 256)
                both = dot(lhl, hi_ref[s, :, c])
                total = both[:n] + both[n:] + dot(lh, lo_ref[s, :, c])
                if vec_ref is not None:
                    vec_out[:, o] = total[:16]
                    total = total[16:]
                oh, ol = split(total)
                out_hi[:, o] = oh
                out_lo[:, o] = ol

    apply_first(khi, klo, kaghi, kaglo, res, kres)
    for copy in first[2]:
        copy.wait_recv()
    hand = pltpu.make_async_remote_copy(
        crows.at[pl.ds(16, 48)], crows.at[pl.ds(80, 48)], ssem0.at[12], rsem0.at[12], around[3], MESH
    )
    hand.start()
    halve(1, 0, shi, slo)
    halve(1, 1, shi, slo)

    apply_first(shi, slo, saghi, saglo, None, None)
    hand.wait_recv()
    h, l = split(crows[...].T)
    cboth[:, 0:128] = h
    cboth[:, 128:256] = l

    fr, _ = factors(0)
    fres[...] = fr
    rho_before = None
    for it in range(ITERS):
        fr = fres[...]
        p = res[...] - product3(fr, aghi[:, :2048], aglo[:, :2048])
        w = kres[...] - product3(fr, kaghi[...], kaglo[...])
        put_blocks(w)
        part = block_sum(w, p)
        going = swap(2 * it)
        spread_out(1 + 2 * it, payload(w, part))
        for copy in going:
            copy.wait_recv()
        for b in range(16):
            zvec[:, b * 128 : b * 128 + 128] = assembled(2 * it, b)
        for s in range(2):
            def store(cols, value):
                szvec[:, cols] = value

            apply(shi, slo, s, zvec[:, s * 1024 : s * 1024 + 1024], store)
        fz, rho = factors(1 + 2 * it)
        y = zvec[...] - product3(fz, aghi[:, :2048], aglo[:, :2048])
        q = szvec[...] - product3(fz, saghi[...], saglo[...])
        if it > 0:
            beta = rho / rho_before
            y = y + beta * dirv[...]
            q = q + beta * qvec[...]
        dirv[...] = y
        qvec[...] = q
        put_blocks(q)
        part = block_sum(q, y)
        going = swap(2 * it + 1)
        spread_out(2 + 2 * it, payload(q, part))
        for copy in going:
            copy.wait_recv()
        for b in range(16):
            zvec[:, b * 128 : b * 128 + 128] = assembled(2 * it + 1, b)
        if it + 1 < ITERS:
            for s in range(2):
                def store(cols, value):
                    szvec[:, cols] = value

                apply(khi, klo, s, zvec[:, s * 1024 : s * 1024 + 1024], store)
        fi, sigma = factors(2 + 2 * it)
        step = rho / sigma
        for s in range(2):
            cols = slice(s * 1024, s * 1024 + 1024)
            add = step * dirv[:, cols]
            if it == 0:
                lam_ref[s] = add
            else:
                lam_ref[s] += add
        res[...] = res[...] - step * zvec[...]
        if it + 1 < ITERS:
            kres[...] = kres[...] - step * szvec[...]
        fres[...] = fres[...] - step * fi
        rho_before = rho

    p = res[...] - product3(fres[...], aghi[:, :2048], aglo[:, :2048])
    for s in range(2):
        out_ref[s] = p[:, s * 1024 : s * 1024 + 1024]

    for copy in first[0] + first[1] + first[2] + [hand] + swaps + mates:
        copy.wait_send()
    for k in range(GATHERS):
        wait_all(ssemg, k)


def hand_over(a_ref, b_ref, c_ref, d_ref):
    c_ref[...] = a_ref[...]
    d_ref[...] = b_ref[...]


def per_device(f_local, schur, precond, modes, coarse_inv, nbr_sub, nbr_blk):
    dma = pltpu.SemaphoreType.DMA
    vec = pltpu.VMEM((16, 2048), F32)
    out = jax.ShapeDtypeStruct((2, 16, 1024), F32)
    anywhere = pl.BlockSpec(memory_space=pl.ANY)
    inside = pl.BlockSpec(memory_space=pltpu.VMEM)
    smem = pl.BlockSpec(memory_space=pltpu.SMEM)
    half = pltpu.VMEM((2, 1024, 1024), BF16)
    tall = pltpu.VMEM((ROWS, 2048), BF16)
    wide = pltpu.VMEM((ROWS, 2176), BF16)
    blocks = pltpu.VMEM((17, 16, 128), F32)
    table = pltpu.SMEM((16,), jnp.int32)
    found = pl.pallas_call(
        kernel,
        out_shape=(out, out),
        in_specs=[smem, smem] + [anywhere] * 5,
        out_specs=(inside,) * 2,
        scratch_shapes=[
            pltpu.VMEM((2, 16, 1024), F32), pltpu.VMEM((6, 2, 1024), F32),
            pltpu.VMEM((12, 1536), F32), pltpu.VMEM((16, 1536), F32), pltpu.VMEM((768, 768), BF16),
            pltpu.VMEM((4, 1024, 1024), F32), half, half, half, half,
            table, table, table, table,
            pltpu.VMEM((16, 16, 128), F32), pltpu.VMEM((17, 16, 128), F32),
            pltpu.VMEM((16, 8, 128), F32), pltpu.VMEM((16, 8, 128), F32), pltpu.VMEM((16, 8, 128), F32),
            pltpu.VMEM((128, 1536), F32), pltpu.VMEM((1536, 256), BF16),
            wide, wide, tall, tall, tall, tall,
            pltpu.VMEM((SWAPS, 16, 16, 128), F32), blocks, blocks, blocks, blocks,
            pltpu.VMEM((16, 16, 128), F32),
            pltpu.VMEM((GATHERS, 5, 64, 2, 128), F32),
            pltpu.VMEM((GATHERS, 16, 128), F32), pltpu.VMEM((GATHERS, 16, 128), F32),
            vec, vec, vec, vec, vec, vec,
            pltpu.VMEM((16, ROWS), F32),
            dma((7,)), dma((13,)), dma((13,)), dma((SWAPS, 4)), dma((SWAPS, 4)),
            dma((GATHERS,)), dma((GATHERS,)), dma((GATHERS,)), dma((GATHERS,)),
        ],
        compiler_params=pltpu.CompilerParams(
            collective_id=0, has_side_effects=True, vmem_limit_bytes=56 * 2**20
        ),
        cost_estimate=pl.CostEstimate(flops=10**9, bytes_accessed=2 * 10**7, transcendentals=0),
    )(nbr_sub, nbr_blk, f_local, schur, precond, modes.transpose(1, 0, 2), coarse_inv)
    return pl.pallas_call(
        hand_over,
        out_shape=(out, out),
        in_specs=[inside] * 2,
        out_specs=(inside,) * 2,
    )(*found)


def solution(mesh):
    flat = P(("sub", "blk"), None)
    tall = P(("sub", "blk"), None, None)
    return jax.shard_map(
        per_device,
        mesh=mesh,
        in_specs=(tall, tall, tall, tall, flat, flat, flat),
        out_specs=(tall, tall),
        check_vma=False,
    )
```

```python
import jax
import jax.numpy as jnp
from jax import lax
from jax.experimental import pallas as pl
from jax.experimental.pallas import tpu as pltpu
from jax.sharding import PartitionSpec as P

ITERS = 2
GATHERS = 1 + 2 * ITERS
SWAPS = 2 * ITERS
NSUB_AX, NBLK_AX = 16, 8
ROWS = 80
BACK = (1, 0, 2, 3)
MESH = pl.DeviceIdType.MESH
F32, BF16 = jnp.float32, jnp.bfloat16


def split(x):
    hi = x.astype(BF16)
    return hi, (x - hi.astype(F32)).astype(BF16)


def dot(a, b):
    return jnp.dot(a, b, preferred_element_type=F32)


def dot_t(a, b):
    return lax.dot_general(a, b, (((1,), (1,)), ((), ())), preferred_element_type=F32)


def product3(x, hi, lo, mul=dot):
    rows = x.shape[0]
    xh, xl = split(x)
    both = mul(jnp.concatenate([xh, xl], axis=0), hi)
    return both[:rows] + both[rows:] + mul(xh, lo)


def kernel(
    nsub_ref, nblk_ref, f_hbm, schur_hbm, precond_hbm, modes_hbm, coarse_hbm,
    lam_ref, out_ref,
    fv, mv, craw, cpad, order, stage, khi, klo, shi, slo,
    group, key, source, pick,
    fsend, frecv, mown, msend, mrecv, crows, cboth,
    aghi, aglo, kaghi, kaglo, saghi, saglo,
    wsend, wrecv0, wrecv1, wrecv2, wrecv3, wblk, gath, fpart, fmate,
    res, kres, zvec, szvec, dirv, qvec, fres, tkhi, tklo, tshi, tslo,
    hsem, ssem0, rsem0, ssemx, rsemx, ssemg, rsemg, ssemf, rsemf,
):
    i, j = lax.axis_index("sub"), lax.axis_index("blk")
    wrecv = (wrecv0, wrecv1, wrecv2, wrecv3)
    yy, xx, zz, cc = i // 4, lax.rem(i, 4), j // 2, lax.rem(j, 2)
    around = [
        (lax.rem(i + 1, NSUB_AX), j),
        (lax.rem(i + NSUB_AX - 1, NSUB_AX), j),
        (i, lax.rem(j + NBLK_AX - 1 + 2 * cc, NBLK_AX)),
        (i, j + 1 - 2 * cc),
    ]
    slot = i * 4 + zz

    def far(q):
        return 2 + (q * (q + 1)) // 2

    columns = [lax.rem(zz + dz, 4) * 2 + cc for dz in (2, 1, 3, 0)]

    def each_chip(act):
        def row(t, carry):
            y = lax.rem(yy + far(t // 4), 4)
            x = lax.rem(xx + far(lax.rem(t, 4)), 4)
            for column in columns:
                act((y * 4 + x, column))
            return carry

        lax.fori_loop(0, 15, row, 0)
        for column in columns[:-1]:
            act((i, column))

    loads = [
        pltpu.make_async_copy(f_hbm, fv, hsem.at[0]),
        pltpu.make_async_copy(modes_hbm, mv, hsem.at[1]),
        pltpu.make_async_copy(coarse_hbm, craw, hsem.at[2]),
    ]
    big = [
        pltpu.make_async_copy(mat.at[s], stage.at[2 * n + s], hsem.at[3 + 2 * n + s])
        for n, mat in enumerate((precond_hbm, schur_hbm))
        for s in range(2)
    ]
    for copy in loads + big:
        copy.start()

    barrier = pltpu.get_barrier_semaphore()

    def greet(where):
        pl.semaphore_signal(barrier, inc=1, device_id=where, device_id_type=MESH)

    each_chip(greet)
    greet(around[2])
    greet(around[3])

    def classify(b, carry):
        s, n = nsub_ref[b // 8, lax.rem(b, 8)], nblk_ref[b // 8, lax.rem(b, 8)]
        dev = s // 2
        dsub, dblk = dev // NBLK_AX, lax.rem(dev, NBLK_AX)
        g = jnp.where(
            dsub == around[0][0], 0,
            jnp.where(dsub == around[1][0], 1, jnp.where(dblk == around[2][1], 2, 3)),
        )
        theirs = lax.rem(s, 2) * 8 + n
        g = jnp.where(s < 0, 4, g)
        group[b] = jnp.where(s < 0, 8, 2 * g + lax.rem(s, 2))
        mine = (g == 0) | (g == 4) | ((g >= 2) & (cc == 0))
        key[b] = g * 16 + jnp.where(mine, b, theirs)
        return carry

    lax.fori_loop(0, 16, classify, 0)

    def rank(b, carry):
        mine = key[b]
        g = mine // 16

        def count(o, slot):
            k = key[o]
            return slot + jnp.where((k < mine) & (k // 16 == g), 1, 0)

        slot = lax.fori_loop(0, 16, count, jnp.int32(0), unroll=True)
        source[b] = jnp.where(g == 4, 16, g * 4 + jnp.minimum(slot, 3))
        return carry

    lax.fori_loop(0, 16, rank, 0)

    def invert(t, carry):
        def match(b, found):
            return jnp.where(source[b] == t, b, found)

        pick[t] = lax.fori_loop(0, 16, match, jnp.int32(0), unroll=True)
        return carry

    lax.fori_loop(0, 16, invert, 0)

    for copy in loads:
        copy.wait()

    zero = jnp.zeros((8, 128), F32)
    pad = jnp.zeros((2, 128), F32)
    for b in range(16):
        s, cols = b // 8, slice((b % 8) * 128, (b % 8) * 128 + 128)
        wide = slice(b * 128, b * 128 + 128)
        wblk[b] = fv[s, :, cols]
        m8 = jnp.concatenate([mv[:, s, cols], pad], axis=0)
        mown[b] = m8
        rows = jnp.concatenate([m8, zero] if s == 0 else [zero, m8], axis=0)
        h, l = split(rows)
        aghi[0:16, wide] = h
        aglo[0:16, wide] = l
    col = lax.broadcasted_iota(jnp.int32, (1, 768), 1)
    spot = lax.rem(col, 128)
    wanted = 16 * lax.rem(spot // 8, 8) + 4 * lax.rem(spot // 2, 4) + 2 * (spot // 64)
    wanted = 6 * (wanted + lax.rem(spot, 2)) + col // 128
    for n in range(6):
        rows = slice(n * 128, n * 128 + 128)
        here = lax.broadcasted_iota(jnp.int32, (128, 768), 0) + n * 128
        order[rows] = jnp.where(here == wanted, 1.0, 0.0).astype(BF16)
    cpad[...] = jnp.zeros((16, 1536), F32)
    cpad[0:6] = craw[0:6]
    cpad[8:14] = craw[6:12]
    for h in range(2):
        cols = slice(768 * h, 768 * h + 768)
        ch, cl = split(cpad[:, cols])
        both = dot(jnp.concatenate([ch, cl], axis=0), order[...])
        crows[0:16, cols] = both[:16] + both[16:]
    row = lax.broadcasted_iota(jnp.int32, (ROWS, 128), 0)
    for n, at in enumerate((6, 7, 14)):
        aghi[:, 2048 + 128 * n : 2176 + 128 * n] = jnp.where(row == at, 1.0, 0.0).astype(BF16)
    aglo[:, 2048:2432] = jnp.zeros((ROWS, 384), BF16)
    for t in range(16):
        fsend[t] = wblk[pick[t]]
        msend[t] = mown[pick[t]]
    frecv[16] = jnp.zeros((16, 128), F32)
    for buf in wrecv:
        buf[16] = jnp.zeros((16, 128), F32)

    def halve(n, s, hi_ref, lo_ref):
        def step(t, carry):
            rows = pl.ds(pl.multiple_of(t * 64, 64), 64)
            h, l = split(stage[2 * n + s, rows])
            hi_ref[s, rows] = h
            lo_ref[s, rows] = l
            return carry

        big[2 * n + s].wait()
        lax.fori_loop(0, 16, step, 0, unroll=2)

    pl.semaphore_wait(barrier, 65)

    first = [[], [], []]
    sources = ((msend, mrecv, 4), (fsend, frecv, 4), (crows, crows, 16))

    def start_first(n):
        src, dst, size = sources[n]
        for g, where in enumerate(around):
            there = BACK[g]
            if n < 2:
                a, b = src.at[pl.ds(size * g, size)], dst.at[pl.ds(size * there, size)]
            else:
                a, b = src.at[pl.ds(0, 16)], dst.at[pl.ds(16 + 16 * there, 16)]
            copy = pltpu.make_async_remote_copy(
                a, b, ssem0.at[4 * n + g], rsem0.at[4 * n + there], where, MESH
            )
            copy.start()
            first[n].append(copy)

    start_first(0)
    halve(0, 0, khi, klo)
    start_first(1)
    start_first(2)
    halve(0, 1, khi, klo)
    for copy in first[0]:
        copy.wait_recv()
    for b in range(16):
        wide = slice(b * 128, b * 128 + 128)
        theirs = mrecv[lax.rem(source[b], 16)]
        code = group[b]
        for pair in range(4):
            both = jnp.concatenate(
                [jnp.where(code == 2 * pair + s2, -theirs, 0.0) for s2 in range(2)], axis=0
            )
            h, l = split(both)
            rows = slice(16 + 16 * pair, 32 + 16 * pair)
            aghi[rows, wide] = h
            aglo[rows, wide] = l

    lane = lax.broadcasted_iota(jnp.int32, (ROWS, 128), 1)
    own = (lane // 16) == lax.rem(row, 8)

    real = lax.rem(row, 8) < 6
    nothing = jnp.zeros((16, 128), F32)

    def onto(vec, sums):
        sums = list(sums) + [nothing] * (3 - len(sums))
        u = jnp.concatenate([vec] + sums, axis=1)
        uh, ul = split(u)
        uh = jnp.concatenate([uh] * 8, axis=0)
        ul = jnp.concatenate([ul] * 8, axis=0)
        both = dot_t(jnp.concatenate([aghi[...], aglo[...]], axis=0), uh)
        return both[:ROWS] + both[ROWS:] + dot_t(aghi[...], ul)

    def pack(r):
        return jnp.sum(jnp.where(own, r, 0.0).reshape(5, 2, 8, 128), axis=2)

    def times(hi, lo, x):
        xh, xl = split(x)
        both = dot(jnp.concatenate([hi[...], lo[...]], axis=0), xh)
        return both[:ROWS] + both[ROWS:] + dot(hi[...], xl)

    def fold(x):
        return jnp.sum(x, axis=0, keepdims=True)

    def spread_out(k, value):
        mine = gath.at[k, :, slot]
        gath[k, :, slot] = value
        each_chip(
            lambda where: pltpu.make_async_remote_copy(
                mine, mine, ssemg.at[k], rsemg.at[k], where, MESH
            ).start()
        )

    def wait_all(sem, k):
        many = gath.at[k, :, pl.ds(0, 63)]
        pltpu.make_async_copy(many, many, sem.at[k]).wait()

    mates = []

    def factors(k, beside):
        wait_all(rsemg, k)
        mine, plus, minus, along, mate = [gath.at[k, n].reshape(128, 128)[...] for n in range(5)]
        same = mine + jnp.concatenate([plus[120:], plus[:120]], axis=0)
        same = same + jnp.concatenate([minus[8:], minus[:8]], axis=0)
        place = lax.rem(lax.broadcasted_iota(jnp.int32, (128, 128), 0), 8)
        up = jnp.where(place < 6, pltpu.roll(along, 126, 0), pltpu.roll(along, 6, 0))
        down = jnp.where(place >= 2, pltpu.roll(along, 2, 0), pltpu.roll(along, 122, 0))
        other = mate + jnp.where(cc == 0, up, down)
        first_core = jnp.where(cc == 0, same, other)
        last_core = jnp.where(cc == 0, other, same)
        x = jnp.concatenate(
            [first_core[:64], last_core[:64], first_core[64:], last_core[64:]], axis=0
        ).T
        scalar = jnp.sum(x[96:112], axis=1, keepdims=True)
        left = jnp.concatenate(
            [
                jnp.concatenate(
                    [part[16 * m : 16 * m + 16, 128 * h : 128 * h + 128] for h in range(2) for m in range(6)],
                    axis=1,
                )
                for part in split(x)
            ],
            axis=0,
        )
        both = dot(left, cboth[...])
        part = both[:16, :128] + both[16:, :128] + both[:16, 128:]
        part = jnp.where(lane[:16] == 6, scalar, part)
        fpart[k] = part
        copy = pltpu.make_async_remote_copy(
            fpart.at[k], fmate.at[k], ssemf.at[k], rsemf.at[k], around[3], MESH
        )
        copy.start()
        mates.append(copy)
        more = beside()
        copy.wait_recv()
        mates_part = fmate[k]
        total = part + pltpu.roll(mates_part, 64, 1)
        turned = jnp.concatenate([total] * 8, axis=0).T
        return (
            total[:, :ROWS], part[:, 6:7] + mates_part[:, 6:7],
            jnp.where(real, turned[:ROWS], 0.0), turned[6:7] + turned[70:71], more,
        )

    def apply(hi_ref, lo_ref, s, vec, store):
        for q in range(4):
            cols = slice(q * 256, q * 256 + 256)
            store(
                slice(s * 1024 + q * 256, s * 1024 + q * 256 + 256),
                product3(vec, hi_ref[s, :, cols], lo_ref[s, :, cols]),
            )

    swaps = []

    def swap(k):
        for t in range(16):
            wsend[k, t] = wblk[pick[t]]
        copies = []
        for g, where in enumerate(around):
            there = BACK[g]
            copy = pltpu.make_async_remote_copy(
                wsend.at[k, pl.ds(4 * g, 4)], wrecv[k].at[pl.ds(4 * there, 4)],
                ssemx.at[k, g], rsemx.at[k, there], where, MESH,
            )
            copy.start()
            copies.append(copy)
        swaps.extend(copies)
        return copies

    def assembled(k, b):
        return wblk[b] - wrecv[k][source[b]]

    def block_sum(a, b):
        total = a[:, 0:128] * b[:, 0:128]
        for n in range(1, 16):
            cols = slice(n * 128, n * 128 + 128)
            total = total + a[:, cols] * b[:, cols]
        return total

    def put_blocks(x):
        for b in range(16):
            wblk[b] = x[:, b * 128 : b * 128 + 128]

    spread_out(0, pack(onto(jnp.concatenate([wblk[b] for b in range(16)], axis=1), [])))
    for copy in first[1]:
        copy.wait_recv()
    for b in range(16):
        res[:, b * 128 : b * 128 + 128] = wblk[b] - frecv[source[b]]

    def apply_first(hi_ref, lo_ref, out_hi, out_lo, vec_ref, vec_out):
        for s in range(2):
            cols = slice(s * 1024, s * 1024 + 1024)
            ah, al = aghi[:, cols], aglo[:, cols]
            parts_hi, parts_lo = [ah], [al]
            if vec_ref is not None:
                vh, vl = split(vec_ref[:, cols])
                parts_hi, parts_lo = [vh, ah], [vl, al]
            lh = jnp.concatenate(parts_hi, axis=0)
            ll = jnp.concatenate(parts_lo, axis=0)
            n = lh.shape[0]
            lhl = jnp.concatenate([lh, ll], axis=0)
            for q in range(4):
                c = slice(q * 256, q * 256 + 256)
                o = slice(s * 1024 + q * 256, s * 1024 + q * 256 + 256)
                both = dot(lhl, hi_ref[s, :, c])
                total = both[:n] + both[n:] + dot(lh, lo_ref[s, :, c])
                if vec_ref is not None:
                    vec_out[:, o] = total[:16]
                    total = total[16:]
                oh, ol = split(total)
                out_hi[:, o] = oh
                out_lo[:, o] = ol

    apply_first(khi, klo, kaghi, kaglo, res, kres)
    for copy in first[2]:
        copy.wait_recv()
    hand = pltpu.make_async_remote_copy(
        crows.at[pl.ds(16, 48)], crows.at[pl.ds(80, 48)], ssem0.at[12], rsem0.at[12], around[3], MESH
    )
    hand.start()
    halve(1, 0, shi, slo)
    halve(1, 1, shi, slo)

    apply_first(shi, slo, saghi, saglo, None, None)
    hand.wait_recv()
    h, l = split(crows[...].T)
    cboth[:, 0:128] = h
    cboth[:, 128:256] = l

    def coupling(ahi, alo, out_hi, out_lo):
        h, l = aghi[:, :2048], aglo[:, :2048]
        both = dot_t(jnp.concatenate([h, l], axis=0), ahi[...])
        out_hi[...], out_lo[...] = split(both[:ROWS] + both[ROWS:] + dot_t(h, alo[...]))

    def at_start():
        coupling(kaghi, kaglo, tkhi, tklo)
        coupling(saghi, saglo, tshi, tslo)
        return onto(kres[...], [block_sum(kres[...], res[...])])

    def collect(k, going):
        for copy in going:
            copy.wait_recv()
        for b in range(16):
            zvec[:, b * 128 : b * 128 + 128] = assembled(k, b)

    def apply_all(hi_ref, lo_ref):
        def store(cols, value):
            szvec[:, cols] = value

        for s in range(2):
            apply(hi_ref, lo_ref, s, zvec[:, s * 1024 : s * 1024 + 1024], store)

    fr, _, frep, _, g = factors(0, at_start)
    fres[...] = fr
    energy = g[6:7]
    step = rho_row = None

    def advance(it):
        for s in range(2):
            cols = slice(s * 1024, s * 1024 + 1024)
            add = step * dirv[:, cols]
            if it == 0:
                lam_ref[s] = add
            else:
                lam_ref[s] += add
        res[...] = res[...] - step * zvec[...]
        if it + 1 < ITERS:
            kres[...] = kres[...] - step * szvec[...]

    for it in range(ITERS):
        if it > 0:
            advance(it - 1)
        put_blocks(kres[...] - product3(fres[...], kaghi[...], kaglo[...]))
        going = swap(2 * it)
        u = g - times(tkhi, tklo, frep)
        scalar = energy - fold(frep * (g + u))
        u = jnp.where(real, u, 0.0)
        spread_out(1 + 2 * it, pack(jnp.where(row == 6, scalar, u)))
        collect(2 * it, going)
        apply_all(shi, slo)

        def beside():
            sums = [block_sum(zvec[...], szvec[...])]
            if it > 0:
                sums.append(block_sum(zvec[...], qvec[...]))
            return onto(szvec[...], sums)

        rho_before = rho_row
        if it > 0:
            rho_col = rho
        fz, rho, frz, rho_row, g2 = factors(1 + 2 * it, beside)
        going = None

        def exchange():
            q = szvec[...] - product3(fz, saghi[...], saglo[...])
            if it > 0:
                q = q + (rho / rho_col) * qvec[...]
            qvec[...] = q
            put_blocks(q)
            return swap(2 * it + 1)

        if it + 1 < ITERS:
            going = exchange()
        u = g2 - times(tshi, tslo, frz)
        scalar = g2[6:7] - fold(frz * (g2 + u))
        u = jnp.where(real, u, 0.0)
        if it > 0:
            beta = rho_row / rho_before
            scalar = scalar + 2 * beta * (g2[7:8] - fold(frz * uq)) + beta * beta * bend
            u = u + beta * uq
        uq, bend = u, scalar
        spread_out(2 + 2 * it, pack(jnp.where(row == 6, scalar, u)))
        if it + 1 == ITERS:
            going = exchange()
        y = zvec[...] - product3(fz, aghi[:, :2048], aglo[:, :2048])
        if it > 0:
            y = y + (rho / rho_col) * dirv[...]
        dirv[...] = y
        collect(2 * it + 1, going)
        if it + 1 < ITERS:
            apply_all(khi, klo)

        def beside():
            if it + 1 == ITERS:
                return None
            return onto(
                szvec[...], [block_sum(szvec[...], res[...]), block_sum(szvec[...], zvec[...])]
            )

        fi, sigma, fri, sigma_row, g3 = factors(2 + 2 * it, beside)
        step, step_row = rho / sigma, rho_row / sigma_row
        fres[...] = fres[...] - step * fi
        if it + 1 < ITERS:
            frep = frep - step_row * fri
            energy = energy - 2 * step_row * g3[6:7] + step_row * step_row * g3[7:8]
            g = g - step_row * g3

    advance(ITERS - 1)
    p = res[...] - product3(fres[...], aghi[:, :2048], aglo[:, :2048])
    for s in range(2):
        out_ref[s] = p[:, s * 1024 : s * 1024 + 1024]

    for copy in first[0] + first[1] + first[2] + [hand] + swaps + mates:
        copy.wait_send()
    for k in range(GATHERS):
        wait_all(ssemg, k)


def hand_over(a_ref, b_ref, c_ref, d_ref):
    c_ref[...] = a_ref[...]
    d_ref[...] = b_ref[...]


def per_device(f_local, schur, precond, modes, coarse_inv, nbr_sub, nbr_blk):
    dma = pltpu.SemaphoreType.DMA
    vec = pltpu.VMEM((16, 2048), F32)
    out = jax.ShapeDtypeStruct((2, 16, 1024), F32)
    anywhere = pl.BlockSpec(memory_space=pl.ANY)
    inside = pl.BlockSpec(memory_space=pltpu.VMEM)
    smem = pl.BlockSpec(memory_space=pltpu.SMEM)
    half = pltpu.VMEM((2, 1024, 1024), BF16)
    tall = pltpu.VMEM((ROWS, 2048), BF16)
    wide = pltpu.VMEM((ROWS, 2432), BF16)
    small = pltpu.VMEM((ROWS, ROWS), BF16)
    blocks = pltpu.VMEM((17, 16, 128), F32)
    table = pltpu.SMEM((16,), jnp.int32)
    found = pl.pallas_call(
        kernel,
        out_shape=(out, out),
        in_specs=[smem, smem] + [anywhere] * 5,
        out_specs=(inside,) * 2,
        scratch_shapes=[
            pltpu.VMEM((2, 16, 1024), F32), pltpu.VMEM((6, 2, 1024), F32),
            pltpu.VMEM((12, 1536), F32), pltpu.VMEM((16, 1536), F32), pltpu.VMEM((768, 768), BF16),
            pltpu.VMEM((4, 1024, 1024), F32), half, half, half, half,
            table, table, table, table,
            pltpu.VMEM((16, 16, 128), F32), pltpu.VMEM((17, 16, 128), F32),
            pltpu.VMEM((16, 8, 128), F32), pltpu.VMEM((16, 8, 128), F32), pltpu.VMEM((16, 8, 128), F32),
            pltpu.VMEM((128, 1536), F32), pltpu.VMEM((1536, 256), BF16),
            wide, wide, tall, tall, tall, tall,
            pltpu.VMEM((SWAPS, 16, 16, 128), F32), blocks, blocks, blocks, blocks,
            pltpu.VMEM((16, 16, 128), F32),
            pltpu.VMEM((GATHERS, 5, 64, 2, 128), F32),
            pltpu.VMEM((GATHERS, 16, 128), F32), pltpu.VMEM((GATHERS, 16, 128), F32),
            vec, vec, vec, vec, vec, vec,
            pltpu.VMEM((16, ROWS), F32), small, small, small, small,
            dma((7,)), dma((13,)), dma((13,)), dma((SWAPS, 4)), dma((SWAPS, 4)),
            dma((GATHERS,)), dma((GATHERS,)), dma((GATHERS,)), dma((GATHERS,)),
        ],
        compiler_params=pltpu.CompilerParams(
            collective_id=0, has_side_effects=True, vmem_limit_bytes=56 * 2**20
        ),
        cost_estimate=pl.CostEstimate(flops=10**9, bytes_accessed=2 * 10**7, transcendentals=0),
    )(nbr_sub, nbr_blk, f_local, schur, precond, modes.transpose(1, 0, 2), coarse_inv)
    return pl.pallas_call(
        hand_over,
        out_shape=(out, out),
        in_specs=[inside] * 2,
        out_specs=(inside,) * 2,
    )(*found)


def solution(mesh):
    flat = P(("sub", "blk"), None)
    tall = P(("sub", "blk"), None, None)
    return jax.shard_map(
        per_device,
        mesh=mesh,
        in_specs=(tall, tall, tall, tall, flat, flat, flat),
        out_specs=(tall, tall),
        check_vma=False,
    )
```

```python
import jax
import jax.numpy as jnp
from jax import lax
from jax.experimental import pallas as pl
from jax.experimental.pallas import tpu as pltpu
from jax.sharding import PartitionSpec as P

ITERS = 2
GATHERS = 1 + 2 * ITERS
SWAPS = 2 * ITERS
NSUB_AX, NBLK_AX = 16, 8
ROWS = 80
BACK = (1, 0, 2, 3)
MESH = pl.DeviceIdType.MESH
F32, BF16 = jnp.float32, jnp.bfloat16


def split(x):
    hi = x.astype(BF16)
    return hi, (x - hi.astype(F32)).astype(BF16)


def dot(a, b):
    return jnp.dot(a, b, preferred_element_type=F32)


def dot_t(a, b):
    return lax.dot_general(a, b, (((1,), (1,)), ((), ())), preferred_element_type=F32)


def product3(x, hi, lo, mul=dot):
    rows = x.shape[0]
    xh, xl = split(x)
    both = mul(jnp.concatenate([xh, xl], axis=0), hi)
    return both[:rows] + both[rows:] + mul(xh, lo)


def kernel(
    nsub_ref, nblk_ref, f_hbm, schur_hbm, precond_hbm, modes_hbm, coarse_hbm,
    lam_ref, out_ref,
    fv, mv, craw, cpad, order, stage, khi, klo, shi, slo,
    group, key, source, pick,
    fsend, frecv, mown, msend, mrecv, crows, cboth,
    aghi, aglo, kaghi, kaglo, saghi, saglo,
    wsend, wrecv0, wrecv1, wrecv2, wrecv3, wblk, gath, fpart, fmate,
    res, kres, zvec, szvec, dirv, qvec, fres,
    hsem, ssem0, rsem0, ssemx, rsemx, ssemg, rsemg, ssemf, rsemf,
):
    i, j = lax.axis_index("sub"), lax.axis_index("blk")
    wrecv = (wrecv0, wrecv1, wrecv2, wrecv3)
    yy, xx, zz, cc = i // 4, lax.rem(i, 4), j // 2, lax.rem(j, 2)
    around = [
        (lax.rem(i + 1, NSUB_AX), j),
        (lax.rem(i + NSUB_AX - 1, NSUB_AX), j),
        (i, lax.rem(j + NBLK_AX - 1 + 2 * cc, NBLK_AX)),
        (i, j + 1 - 2 * cc),
    ]
    slot = i * 4 + zz

    def far(q):
        return 2 + (q * (q + 1)) // 2

    columns = [lax.rem(zz + dz, 4) * 2 + cc for dz in (2, 1, 3, 0)]

    def each_chip(act):
        def row(t, carry):
            y = lax.rem(yy + far(t // 4), 4)
            x = lax.rem(xx + far(lax.rem(t, 4)), 4)
            for column in columns:
                act((y * 4 + x, column))
            return carry

        lax.fori_loop(0, 15, row, 0)
        for column in columns[:-1]:
            act((i, column))

    loads = [
        pltpu.make_async_copy(f_hbm, fv, hsem.at[0]),
        pltpu.make_async_copy(modes_hbm, mv, hsem.at[1]),
        pltpu.make_async_copy(coarse_hbm, craw, hsem.at[2]),
    ]
    big = [
        pltpu.make_async_copy(mat.at[s], stage.at[2 * n + s], hsem.at[3 + 2 * n + s])
        for n, mat in enumerate((precond_hbm, schur_hbm))
        for s in range(2)
    ]
    for copy in loads + big:
        copy.start()

    barrier = pltpu.get_barrier_semaphore()

    def greet(where):
        pl.semaphore_signal(barrier, inc=1, device_id=where, device_id_type=MESH)

    each_chip(greet)
    greet(around[2])
    greet(around[3])

    def classify(b, carry):
        s, n = nsub_ref[b // 8, lax.rem(b, 8)], nblk_ref[b // 8, lax.rem(b, 8)]
        dev = s // 2
        dsub, dblk = dev // NBLK_AX, lax.rem(dev, NBLK_AX)
        g = jnp.where(
            dsub == around[0][0], 0,
            jnp.where(dsub == around[1][0], 1, jnp.where(dblk == around[2][1], 2, 3)),
        )
        theirs = lax.rem(s, 2) * 8 + n
        g = jnp.where(s < 0, 4, g)
        group[b] = jnp.where(s < 0, 8, 2 * g + lax.rem(s, 2))
        mine = (g == 0) | (g == 4) | ((g >= 2) & (cc == 0))
        key[b] = g * 16 + jnp.where(mine, b, theirs)
        return carry

    lax.fori_loop(0, 16, classify, 0)

    def rank(b, carry):
        mine = key[b]
        g = mine // 16

        def count(o, slot):
            k = key[o]
            return slot + jnp.where((k < mine) & (k // 16 == g), 1, 0)

        slot = lax.fori_loop(0, 16, count, jnp.int32(0), unroll=True)
        source[b] = jnp.where(g == 4, 16, g * 4 + jnp.minimum(slot, 3))
        return carry

    lax.fori_loop(0, 16, rank, 0)

    def invert(t, carry):
        def match(b, found):
            return jnp.where(source[b] == t, b, found)

        pick[t] = lax.fori_loop(0, 16, match, jnp.int32(0), unroll=True)
        return carry

    lax.fori_loop(0, 16, invert, 0)

    for copy in loads:
        copy.wait()

    zero = jnp.zeros((8, 128), F32)
    pad = jnp.zeros((2, 128), F32)
    for b in range(16):
        s, cols = b // 8, slice((b % 8) * 128, (b % 8) * 128 + 128)
        wide = slice(b * 128, b * 128 + 128)
        wblk[b] = fv[s, :, cols]
        m8 = jnp.concatenate([mv[:, s, cols], pad], axis=0)
        mown[b] = m8
        rows = jnp.concatenate([m8, zero] if s == 0 else [zero, m8], axis=0)
        h, l = split(rows)
        aghi[0:16, wide] = h
        aglo[0:16, wide] = l
    col = lax.broadcasted_iota(jnp.int32, (1, 768), 1)
    spot = lax.rem(col, 128)
    wanted = 16 * lax.rem(spot // 8, 8) + 4 * lax.rem(spot // 2, 4) + 2 * (spot // 64)
    wanted = 6 * (wanted + lax.rem(spot, 2)) + col // 128
    for n in range(6):
        rows = slice(n * 128, n * 128 + 128)
        here = lax.broadcasted_iota(jnp.int32, (128, 768), 0) + n * 128
        order[rows] = jnp.where(here == wanted, 1.0, 0.0).astype(BF16)
    cpad[...] = jnp.zeros((16, 1536), F32)
    cpad[0:6] = craw[0:6]
    cpad[8:14] = craw[6:12]
    for h in range(2):
        cols = slice(768 * h, 768 * h + 768)
        ch, cl = split(cpad[:, cols])
        both = dot(jnp.concatenate([ch, cl], axis=0), order[...])
        crows[0:16, cols] = both[:16] + both[16:]
    row = lax.broadcasted_iota(jnp.int32, (ROWS, 128), 0)
    aghi[:, 2048:2176] = jnp.where(row == 6, 1.0, 0.0).astype(BF16)
    aglo[:, 2048:2176] = jnp.zeros((ROWS, 128), BF16)
    for t in range(16):
        fsend[t] = wblk[pick[t]]
        msend[t] = mown[pick[t]]
    frecv[16] = jnp.zeros((16, 128), F32)
    for buf in wrecv:
        buf[16] = jnp.zeros((16, 128), F32)

    def halve(n, s, hi_ref, lo_ref):
        def step(t, carry):
            rows = pl.ds(pl.multiple_of(t * 64, 64), 64)
            h, l = split(stage[2 * n + s, rows])
            hi_ref[s, rows] = h
            lo_ref[s, rows] = l
            return carry

        big[2 * n + s].wait()
        lax.fori_loop(0, 16, step, 0, unroll=2)

    pl.semaphore_wait(barrier, 65)

    first = [[], [], []]
    sources = ((msend, mrecv, 4), (fsend, frecv, 4), (crows, crows, 16))

    def start_first(n):
        src, dst, size = sources[n]
        for g, where in enumerate(around):
            there = BACK[g]
            if n < 2:
                a, b = src.at[pl.ds(size * g, size)], dst.at[pl.ds(size * there, size)]
            else:
                a, b = src.at[pl.ds(0, 16)], dst.at[pl.ds(16 + 16 * there, 16)]
            copy = pltpu.make_async_remote_copy(
                a, b, ssem0.at[4 * n + g], rsem0.at[4 * n + there], where, MESH
            )
            copy.start()
            first[n].append(copy)

    start_first(0)
    halve(0, 0, khi, klo)
    start_first(1)
    start_first(2)
    halve(0, 1, khi, klo)
    for copy in first[0]:
        copy.wait_recv()
    for b in range(16):
        wide = slice(b * 128, b * 128 + 128)
        theirs = mrecv[lax.rem(source[b], 16)]
        code = group[b]
        for pair in range(4):
            both = jnp.concatenate(
                [jnp.where(code == 2 * pair + s2, -theirs, 0.0) for s2 in range(2)], axis=0
            )
            h, l = split(both)
            rows = slice(16 + 16 * pair, 32 + 16 * pair)
            aghi[rows, wide] = h
            aglo[rows, wide] = l

    lane = lax.broadcasted_iota(jnp.int32, (ROWS, 128), 1)
    own = (lane // 16) == lax.rem(row, 8)

    def payload(vec, scalar):
        u = jnp.concatenate([vec, scalar], axis=1)
        uh, ul = split(u)
        uh = jnp.concatenate([uh] * 8, axis=0)
        ul = jnp.concatenate([ul] * 8, axis=0)
        both = dot_t(jnp.concatenate([aghi[...], aglo[...]], axis=0), uh)
        r = both[:ROWS] + both[ROWS:] + dot_t(aghi[...], ul)
        r = jnp.where(own, r, 0.0)
        return jnp.sum(r.reshape(5, 2, 8, 128), axis=2)

    def spread_out(k, value):
        mine = gath.at[k, :, slot]
        gath[k, :, slot] = value
        each_chip(
            lambda where: pltpu.make_async_remote_copy(
                mine, mine, ssemg.at[k], rsemg.at[k], where, MESH
            ).start()
        )

    def wait_all(sem, k):
        many = gath.at[k, :, pl.ds(0, 63)]
        pltpu.make_async_copy(many, many, sem.at[k]).wait()

    mates = []

    def factors(k):
        wait_all(rsemg, k)
        mine, plus, minus, along, mate = [gath.at[k, n].reshape(128, 128)[...] for n in range(5)]
        same = mine + jnp.concatenate([plus[120:], plus[:120]], axis=0)
        same = same + jnp.concatenate([minus[8:], minus[:8]], axis=0)
        place = lax.rem(lax.broadcasted_iota(jnp.int32, (128, 128), 0), 8)
        up = jnp.where(place < 6, pltpu.roll(along, 126, 0), pltpu.roll(along, 6, 0))
        down = jnp.where(place >= 2, pltpu.roll(along, 2, 0), pltpu.roll(along, 122, 0))
        other = mate + jnp.where(cc == 0, up, down)
        first_core = jnp.where(cc == 0, same, other)
        last_core = jnp.where(cc == 0, other, same)
        x = jnp.concatenate(
            [first_core[:64], last_core[:64], first_core[64:], last_core[64:]], axis=0
        ).T
        scalar = jnp.sum(x[96:112], axis=1, keepdims=True)
        left = jnp.concatenate(
            [
                jnp.concatenate(
                    [part[16 * m : 16 * m + 16, 128 * h : 128 * h + 128] for h in range(2) for m in range(6)],
                    axis=1,
                )
                for part in split(x)
            ],
            axis=0,
        )
        both = dot(left, cboth[...])
        part = both[:16, :128] + both[16:, :128] + both[:16, 128:]
        part = jnp.where(lane[:16] == 6, scalar, part)
        fpart[k] = part
        copy = pltpu.make_async_remote_copy(
            fpart.at[k], fmate.at[k], ssemf.at[k], rsemf.at[k], around[3], MESH
        )
        copy.start()
        mates.append(copy)
        copy.wait_recv()
        mates_part = fmate[k]
        total = part + pltpu.roll(mates_part, 64, 1)
        return total[:, :ROWS], part[:, 6:7] + mates_part[:, 6:7]

    def apply(hi_ref, lo_ref, s, vec, store):
        for q in range(4):
            cols = slice(q * 256, q * 256 + 256)
            store(
                slice(s * 1024 + q * 256, s * 1024 + q * 256 + 256),
                product3(vec, hi_ref[s, :, cols], lo_ref[s, :, cols]),
            )

    swaps = []

    def swap(k):
        for t in range(16):
            wsend[k, t] = wblk[pick[t]]
        copies = []
        for g, where in enumerate(around):
            there = BACK[g]
            copy = pltpu.make_async_remote_copy(
                wsend.at[k, pl.ds(4 * g, 4)], wrecv[k].at[pl.ds(4 * there, 4)],
                ssemx.at[k, g], rsemx.at[k, there], where, MESH,
            )
            copy.start()
            copies.append(copy)
        swaps.extend(copies)
        return copies

    def assembled(k, b):
        return wblk[b] - wrecv[k][source[b]]

    def block_sum(a, b):
        total = a[:, 0:128] * b[:, 0:128]
        for n in range(1, 16):
            cols = slice(n * 128, n * 128 + 128)
            total = total + a[:, cols] * b[:, cols]
        return total

    def put_blocks(x):
        for b in range(16):
            wblk[b] = x[:, b * 128 : b * 128 + 128]

    spread_out(0, payload(jnp.concatenate([wblk[b] for b in range(16)], axis=1), jnp.zeros((16, 128), F32)))
    for copy in first[1]:
        copy.wait_recv()
    for b in range(16):
        res[:, b * 128 : b * 128 + 128] = wblk[b] - frecv[source[b]]

    def apply_first(hi_ref, lo_ref, out_hi, out_lo, vec_ref, vec_out):
        for s in range(2):
            cols = slice(s * 1024, s * 1024 + 1024)
            ah, al = aghi[:, cols], aglo[:, cols]
            parts_hi, parts_lo = [ah], [al]
            if vec_ref is not None:
                vh, vl = split(vec_ref[:, cols])
                parts_hi, parts_lo = [vh, ah], [vl, al]
            lh = jnp.concatenate(parts_hi, axis=0)
            ll = jnp.concatenate(parts_lo, axis=0)
            n = lh.shape[0]
            lhl = jnp.concatenate([lh, ll], axis=0)
            for q in range(4):
                c = slice(q * 256, q * 256 + 256)
                o = slice(s * 1024 + q * 256, s * 1024 + q * 256 + 256)
                both = dot(lhl, hi_ref[s, :, c])
                total = both[:n] + both[n:] + dot(lh, lo_ref[s, :, c])
                if vec_ref is not None:
                    vec_out[:, o] = total[:16]
                    total = total[16:]
                oh, ol = split(total)
                out_hi[:, o] = oh
                out_lo[:, o] = ol

    apply_first(khi, klo, kaghi, kaglo, res, kres)
    for copy in first[2]:
        copy.wait_recv()
    hand = pltpu.make_async_remote_copy(
        crows.at[pl.ds(16, 48)], crows.at[pl.ds(80, 48)], ssem0.at[12], rsem0.at[12], around[3], MESH
    )
    hand.start()
    halve(1, 0, shi, slo)
    halve(1, 1, shi, slo)

    apply_first(shi, slo, saghi, saglo, None, None)
    hand.wait_recv()
    h, l = split(crows[...].T)
    cboth[:, 0:128] = h
    cboth[:, 128:256] = l

    fr, _ = factors(0)
    fres[...] = fr
    rho_before = None
    for it in range(ITERS):
        fr = fres[...]
        p = res[...] - product3(fr, aghi[:, :2048], aglo[:, :2048])
        w = kres[...] - product3(fr, kaghi[...], kaglo[...])
        put_blocks(w)
        part = block_sum(w, p)
        going = swap(2 * it)
        spread_out(1 + 2 * it, payload(w, part))
        for copy in going:
            copy.wait_recv()
        for b in range(16):
            zvec[:, b * 128 : b * 128 + 128] = assembled(2 * it, b)
        for s in range(2):
            def store(cols, value):
                szvec[:, cols] = value

            apply(shi, slo, s, zvec[:, s * 1024 : s * 1024 + 1024], store)
        fz, rho = factors(1 + 2 * it)
        y = zvec[...] - product3(fz, aghi[:, :2048], aglo[:, :2048])
        q = szvec[...] - product3(fz, saghi[...], saglo[...])
        if it > 0:
            beta = rho / rho_before
            y = y + beta * dirv[...]
            q = q + beta * qvec[...]
        dirv[...] = y
        qvec[...] = q
        put_blocks(q)
        part = block_sum(q, y)
        if it + 1 < ITERS:
            going = swap(2 * it + 1)
        spread_out(2 + 2 * it, payload(q, part))
        if it + 1 == ITERS:
            going = swap(2 * it + 1)
        for copy in going:
            copy.wait_recv()
        for b in range(16):
            zvec[:, b * 128 : b * 128 + 128] = assembled(2 * it + 1, b)
        if it + 1 < ITERS:
            for s in range(2):
                def store(cols, value):
                    szvec[:, cols] = value

                apply(khi, klo, s, zvec[:, s * 1024 : s * 1024 + 1024], store)
        fi, sigma = factors(2 + 2 * it)
        step = rho / sigma
        for s in range(2):
            cols = slice(s * 1024, s * 1024 + 1024)
            add = step * dirv[:, cols]
            if it == 0:
                lam_ref[s] = add
            else:
                lam_ref[s] += add
        res[...] = res[...] - step * zvec[...]
        if it + 1 < ITERS:
            kres[...] = kres[...] - step * szvec[...]
        fres[...] = fres[...] - step * fi
        rho_before = rho

    p = res[...] - product3(fres[...], aghi[:, :2048], aglo[:, :2048])
    for s in range(2):
        out_ref[s] = p[:, s * 1024 : s * 1024 + 1024]

    for copy in first[0] + first[1] + first[2] + [hand] + swaps + mates:
        copy.wait_send()
    for k in range(GATHERS):
        wait_all(ssemg, k)


def hand_over(a_ref, b_ref, c_ref, d_ref):
    c_ref[...] = a_ref[...]
    d_ref[...] = b_ref[...]


def per_device(f_local, schur, precond, modes, coarse_inv, nbr_sub, nbr_blk):
    dma = pltpu.SemaphoreType.DMA
    vec = pltpu.VMEM((16, 2048), F32)
    out = jax.ShapeDtypeStruct((2, 16, 1024), F32)
    anywhere = pl.BlockSpec(memory_space=pl.ANY)
    inside = pl.BlockSpec(memory_space=pltpu.VMEM)
    smem = pl.BlockSpec(memory_space=pltpu.SMEM)
    half = pltpu.VMEM((2, 1024, 1024), BF16)
    tall = pltpu.VMEM((ROWS, 2048), BF16)
    wide = pltpu.VMEM((ROWS, 2176), BF16)
    blocks = pltpu.VMEM((17, 16, 128), F32)
    table = pltpu.SMEM((16,), jnp.int32)
    found = pl.pallas_call(
        kernel,
        out_shape=(out, out),
        in_specs=[smem, smem] + [anywhere] * 5,
        out_specs=(inside,) * 2,
        scratch_shapes=[
            pltpu.VMEM((2, 16, 1024), F32), pltpu.VMEM((6, 2, 1024), F32),
            pltpu.VMEM((12, 1536), F32), pltpu.VMEM((16, 1536), F32), pltpu.VMEM((768, 768), BF16),
            pltpu.VMEM((4, 1024, 1024), F32), half, half, half, half,
            table, table, table, table,
            pltpu.VMEM((16, 16, 128), F32), pltpu.VMEM((17, 16, 128), F32),
            pltpu.VMEM((16, 8, 128), F32), pltpu.VMEM((16, 8, 128), F32), pltpu.VMEM((16, 8, 128), F32),
            pltpu.VMEM((128, 1536), F32), pltpu.VMEM((1536, 256), BF16),
            wide, wide, tall, tall, tall, tall,
            pltpu.VMEM((SWAPS, 16, 16, 128), F32), blocks, blocks, blocks, blocks,
            pltpu.VMEM((16, 16, 128), F32),
            pltpu.VMEM((GATHERS, 5, 64, 2, 128), F32),
            pltpu.VMEM((GATHERS, 16, 128), F32), pltpu.VMEM((GATHERS, 16, 128), F32),
            vec, vec, vec, vec, vec, vec,
            pltpu.VMEM((16, ROWS), F32),
            dma((7,)), dma((13,)), dma((13,)), dma((SWAPS, 4)), dma((SWAPS, 4)),
            dma((GATHERS,)), dma((GATHERS,)), dma((GATHERS,)), dma((GATHERS,)),
        ],
        compiler_params=pltpu.CompilerParams(
            collective_id=0, has_side_effects=True, vmem_limit_bytes=56 * 2**20
        ),
        cost_estimate=pl.CostEstimate(flops=10**9, bytes_accessed=2 * 10**7, transcendentals=0),
    )(nbr_sub, nbr_blk, f_local, schur, precond, modes.transpose(1, 0, 2), coarse_inv)
    return pl.pallas_call(
        hand_over,
        out_shape=(out, out),
        in_specs=[inside] * 2,
        out_specs=(inside,) * 2,
    )(*found)


def solution(mesh):
    flat = P(("sub", "blk"), None)
    tall = P(("sub", "blk"), None, None)
    return jax.shard_map(
        per_device,
        mesh=mesh,
        in_specs=(tall, tall, tall, tall, flat, flat, flat),
        out_specs=(tall, tall),
        check_vma=False,
    )
```
